256 devices in a mesh: rows: 32 (over x, z_hi, core), cols: 8 (over z_lo, y).
Axes of the slice: x: 4, y: 4, z: 8 (z_hi: 4, z_lo: 2; z = z_hi * 2 + z_lo), core: 2. Of those that a mesh axis runs over, the one named last changes fastest.
Arguments:
- cell_cost: float32 [256, 4096], P('rows', 'cols'), may hold values from 0.2 to 8, as said below
- blocked: int32 [256, 4096], P('rows', 'cols'), may hold values 0 or 1
- move_table: int32 [8, 8], replicated, may hold values from 0 to 7
- anchor_cells: int32 [32, 8, 128], P('rows', 'cols'), may hold values from 0 to 4095
- anchor_mass: float32 [32, 8, 128], P('rows', 'cols'), may hold values from 0.5 to 2
Outputs:
- values: float32 [8, 256, 4096], P(None, 'rows', 'cols')
- visits: float32 [256, 4096], P('rows', 'cols')
The draws below stay inside these ranges and needn't reach their ends.
Inputs may be any that keep to these rules, and one draw needn't show every extreme that they name: `cell_cost`: positive costs. `anchor_cells`: row-major cell index within the device's own tile.
All inputs are finite; a program needn't handle non-finite values. No bound on the sum of `blocked` on one device may be relied on, other than what follows from the above.
Results may differ from the reference program's by a relative error of at most 0.0003.
Values sent between devices are 32-bit elements; how exact they have to be, the bound alone decides.
No kernel may reach another device: no remote copies, remote signals or barrier semaphores. Data moves between devices by JAX's collectives and lax.ppermute only.
A program may use at most 64 MiB of HBM per device.

```python
import math
import jax
import jax.numpy as jnp
from jax import lax

TR = 8
TC = 512
ITERS = 20
HEADINGS = 8
ANCHORS = 128
NR = 256
NC = 4096
N_ROWS = 32
N_COLS = 8


def draw_cell_cost(key, part):
    spread = jax.random.uniform(key, (NR, NC), jnp.float32, jnp.log(0.2), jnp.log(8.0))
    return jnp.exp(spread)


def plant(drawn, rng, smallest, high):
    place = [jax.random.randint(jax.random.fold_in(rng, axis), (), 0, length) for axis, length in enumerate(drawn.shape)]
    longest = drawn.shape.index(max(drawn.shape))
    neighbour = place[:longest] + [(place[longest] + 1) % drawn.shape[longest]] + place[longest + 1:]
    return drawn.at[tuple(place)].set(smallest).at[tuple(neighbour)].set(high)


def steps_of(key, dims, split, smallest, high):
    def one(axis_at, shards_of):
        steps = jax.random.uniform(jax.random.fold_in(jax.random.fold_in(key, 6), axis_at), (shards_of,), jnp.float32, smallest / len(split), high / len(split))
        return jnp.repeat(jnp.exp(steps), dims[axis_at] // shards_of).reshape((-1,) + (1,) * (len(dims) - axis_at - 1))

    factor_of = one(*split[0])
    for cut in split[1:]:
        factor_of = factor_of * one(*cut)
    return factor_of


def setup_inputs(seed: int = 0) -> dict:
    keys = jax.random.split(jax.random.key(seed), 6)
    cell_cost = draw_cell_cost(jax.random.fold_in(keys[5], 71), 0)
    blocked = plant((jax.random.randint(keys[1], (NR, NC), 0, 20) < 3).astype(jnp.int32), jax.random.fold_in(keys[1], 1), 0, 1)
    move_table = plant(jax.random.randint(keys[2], (HEADINGS, HEADINGS), 0, 8), jax.random.fold_in(keys[2], 1), 0, 7).astype(jnp.int32)
    anchor_cells = plant(jax.random.randint(keys[3], (N_ROWS, N_COLS, ANCHORS), 0, TR * TC), jax.random.fold_in(keys[3], 1), 0, (TR * TC) - 1).astype(jnp.int32)
    anchor_mass = jnp.clip(jnp.exp(math.log(2.0) - 1.3862944 * jax.random.uniform(keys[4], (N_ROWS, N_COLS, ANCHORS), jnp.float32) ** steps_of(keys[4], (N_ROWS, N_COLS, ANCHORS), ((0, 32), (1, 8)), -0.2, 0.2)), 0.5, 2.0)
    return {"cell_cost": cell_cost, "blocked": blocked, "move_table": move_table, "anchor_cells": anchor_cells, "anchor_mass": anchor_mass}


PENALTY = 3.0
ROW_STEP = (0, -1, -1, -1, 0, 1, 1, 1)
COL_STEP = (1, 1, 0, -1, -1, -1, 0, 1)


def successors(value, penalty_pad):
    total_rows = value.shape[1]
    total_cols = value.shape[2]
    padded = jnp.pad(value, ((0, 0), (1, 1), (1, 1)))
    parts = []
    for heading in range(8):
        top = 1 + ROW_STEP[heading]
        left = 1 + COL_STEP[heading]
        parts.append(padded[heading, top:top + total_rows, left:left + total_cols]
                     + penalty_pad[top:top + total_rows, left:left + total_cols])
    return jnp.stack(parts)


def log_total(chosen):
    largest = jnp.max(chosen, axis=0)
    return largest + jnp.log(jnp.sum(jnp.exp(chosen - largest[None]), axis=0))


def reference(cell_cost, blocked, move_table, anchor_cells, anchor_mass):
    total_rows, total_cols = cell_cost.shape
    penalty = -PENALTY * blocked.astype(jnp.float32)
    penalty_pad = jnp.pad(penalty, 1)
    value = jnp.zeros((8, total_rows, total_cols), jnp.float32)
    stored = []
    for turn in range(ITERS):
        stored.append(value)
        shifted = successors(value, penalty_pad)
        totals = lax.map(lambda heading_row: log_total(jnp.take(shifted, heading_row, axis=0)), move_table)
        value = totals - cell_cost[None]
    values = value / ITERS

    tile_rows = jnp.arange(N_ROWS, dtype=jnp.int32)[:, None, None] * TR + anchor_cells // TC
    tile_cols = jnp.arange(N_COLS, dtype=jnp.int32)[None, :, None] * TC + anchor_cells % TC
    start = jnp.zeros((total_rows, total_cols), jnp.float32)
    start = start.at[tile_rows.reshape(-1), tile_cols.reshape(-1)].add(anchor_mass.reshape(-1))
    density = jnp.broadcast_to(start[None] / 8.0, (8, total_rows, total_cols))
    visits = jnp.zeros((total_rows, total_cols), jnp.float32)
    headings = jnp.arange(8, dtype=jnp.int32)
    for turn in range(ITERS):
        shifted = successors(stored[ITERS - 1 - turn], penalty_pad)

        def add_heading(arrivals, inputs):
            heading_row, mass = inputs
            chosen = jnp.take(shifted, heading_row, axis=0)
            policy = jnp.exp(chosen - log_total(chosen)[None])
            selector = (heading_row[None, :] == headings[:, None]).astype(jnp.float32)
            flow = mass[None] * policy
            arrivals = arrivals + jnp.einsum('ka,axy->kxy', selector, flow, precision=lax.Precision.HIGHEST)
            return arrivals, None

        arrivals, unused = lax.scan(add_heading, jnp.zeros((8, total_rows, total_cols), jnp.float32), (move_table, density))
        padded = jnp.pad(arrivals, ((0, 0), (1, 1), (1, 1)))
        parts = []
        for heading in range(8):
            top = 1 - ROW_STEP[heading]
            left = 1 - COL_STEP[heading]
            parts.append(padded[heading, top:top + total_rows, left:left + total_cols])
        density = jnp.stack(parts)
        visits = visits + jnp.sum(density, axis=0)
    return values, visits
```

```python
import functools

import jax
import jax.numpy as jnp
from jax import lax
from jax.experimental import pallas as pl
from jax.experimental.pallas import tpu as pltpu
from jax.sharding import PartitionSpec as P

ITERS = 20
PENALTY = 3.0
ROW_STEP = (0, -1, -1, -1, 0, 1, 1, 1)
COL_STEP = (1, 1, 0, -1, -1, -1, 0, 1)
TR, TC = 8, 512
REACH = 5
EDGE = 64
WIDE = TC + 2 * EDGE
LANES = WIDE // 128
TILES = 2 * REACH + 1
GROUP = 8
Z_SCALE = 2.0**60
Y_SCALE = 2.0**30
Z_FLOOR = 2.0**-36


def prepare_kernel(cost_ref, blocked_ref, cells_ref, mass_ref, out_ref):
    penalty = -PENALTY * blocked_ref[...].astype(jnp.float32)
    out_ref[0:8] = cost_ref[...] - penalty
    out_ref[8:16] = penalty
    cells = cells_ref[...]
    row = lax.broadcasted_iota(jnp.int32, (TR, 128), 0)
    weight = jnp.where(row == (cells >> 9), mass_ref[...], 0.0)
    col = lax.broadcasted_iota(jnp.int32, (TC, 128), 0)
    hot = jnp.where(col == (cells & (TC - 1)), 1.0, 0.0)
    start = lax.dot_general(
        weight, hot, (((1,), (1,)), ((), ())),
        preferred_element_type=jnp.float32, precision=lax.Precision.HIGHEST,
    )
    out_ref[16:24] = start * 0.125


def take(buf, slot, k, base):
    return jnp.concatenate([buf[slot, k, l, pl.ds(base, 8), :] for l in range(LANES)], axis=1)


def put(buf, slot, k, base, x):
    for l in range(LANES):
        buf[slot, k, l, pl.ds(base, 8), :] = x[:, 128 * l : 128 * l + 128]


def shifted(buf, slot, k, base, sign):
    dr, dc = sign * ROW_STEP[k], sign * COL_STEP[k]
    x = take(buf, slot, k, base + dr)
    return pltpu.roll(x, (-dc) % WIDE, 1) if dc else x


def mix(mat, parts):
    x = jnp.concatenate(parts, axis=0)
    hi = x.astype(jnp.bfloat16)
    lo = (x - hi.astype(jnp.float32)).astype(jnp.bfloat16)
    y = jnp.dot(mat, jnp.concatenate([hi, lo], axis=0), preferred_element_type=jnp.float32)
    return [y[8 * k : 8 * k + 8] for k in range(8)]


def span(radius):
    far = (radius + 7) // 8
    return REACH - far + 1, REACH + far + 2


def main_kernel(
    pos_ref, table_ref, moves_ref, up_ref, mid_ref, down_ref, cost_ref, values_ref, visits_ref,
    damp, outer, start, buf, held, stack, picked, gathered,
):
    pos = pos_ref[0]
    lane = lax.broadcasted_iota(jnp.int32, (8, WIDE), 1)
    sub = lax.broadcasted_iota(jnp.int32, (8, WIDE), 0)
    zero = jnp.zeros((8, WIDE), jnp.float32)
    one = jnp.full((8, WIDE), Z_SCALE, jnp.float32)
    for slot in range(2):
        for k in range(8):
            for edge in (0, TILES + 1):
                put(buf, slot, k, 8 * edge, one)

    def fetch(src, at, tile, raw):
        block = src[at]
        enter, pen, mass = block[0:8], block[8:16], block[16:24]
        base = pl.multiple_of(8 * tile, 8)
        inside = enter > 0.0
        row = 8 * tile + sub - 8 * (REACH + 1)
        near = (row >= -20) & (row < TR + 20) & (lane >= EDGE - 20) & (lane < EDGE + TC + 20)
        start[pl.ds(base, 8), :] = jnp.where(near, mass, 0.0)
        if raw:
            damp[pl.ds(base, 8), :] = enter
            first = pen
        else:
            damp[pl.ds(base, 8), :] = jnp.where(inside, jnp.exp(-enter), 0.0)
            outer[pl.ds(base, 8), :] = jnp.where(inside, 0.0, one)
            first = jnp.exp(pen) * Z_SCALE
        for k in range(8):
            put(buf, 0, k, base, first)
            put(buf, 1, k, base, first)

    def load_window(raw):
        def body(tile, carry):
            at = pos + tile - 1

            @pl.when(at < REACH)
            def _():
                fetch(up_ref, at, tile, raw)

            @pl.when((at >= REACH) & (at < REACH + GROUP))
            def _():
                fetch(mid_ref, at - REACH, tile, raw)

            @pl.when(at >= REACH + GROUP)
            def _():
                fetch(down_ref, at - REACH - GROUP, tile, raw)

            return carry

        lax.fori_loop(1, TILES + 1, body, 0)

    load_window(False)

    table = jnp.broadcast_to(table_ref[...].reshape(8, 1, 8), (8, 8, 8)).reshape(64, 8)
    col = lax.broadcasted_iota(jnp.int32, (64, 64), 1)
    row = lax.broadcasted_iota(jnp.int32, (64, 64), 0)
    count = jnp.zeros((64, 64), jnp.float32)
    for a in range(8):
        count = count + jnp.where(table[:, a : a + 1] == (col >> 3), 1.0, 0.0)
    count = jnp.where((row & 7) == (col & 7), count, 0.0)
    back = jnp.concatenate([count, count], axis=1).astype(jnp.bfloat16)
    turned = count.T
    forth = jnp.concatenate([turned, turned], axis=1).astype(jnp.bfloat16)
    mine = 8 * (REACH + 1)

    def back_step(n, carry):
        t = ITERS - 1 - n
        now, later = n & 1, 1 - (n & 1)
        lo, hi = span(t + 20)

        def tile_step(tile, carry):
            base = pl.multiple_of(8 * tile, 8)
            totals = mix(back, [shifted(buf, now, k, base, 1) for k in range(8)])
            e, o = damp[pl.ds(base, 8), :], outer[pl.ds(base, 8), :]
            for k in range(8):
                put(buf, later, k, base, totals[k] * e + o)

            @pl.when(tile == REACH + 1)
            def _():
                for k in range(8):
                    held[t, k] = totals[k]

            return carry

        lax.fori_loop(lo, hi, tile_step, carry)
        return carry

    lax.fori_loop(0, ITERS - 1, back_step, 0)
    now, later = (ITERS - 1) & 1, 1 - ((ITERS - 1) & 1)
    lo, hi = span(20)

    def turn_step(tile, least):
        base = pl.multiple_of(8 * tile, 8)
        totals = mix(back, [shifted(buf, now, k, base, 1) for k in range(8)])
        mass = start[pl.ds(base, 8), :]
        low = totals[0]
        for k in range(1, 8):
            low = jnp.minimum(low, totals[k])
        row = 8 * tile + sub - mine
        near = (row >= -20) & (row < TR + 20) & (lane >= EDGE - 20) & (lane < EDGE + TC + 20)
        live = near & (damp[pl.ds(base, 8), :] > 0.0)
        least = jnp.minimum(least, jnp.where(live, low, Z_SCALE))
        flow = mix(forth, [jnp.where(live & (mass > 0.0), mass * (Y_SCALE / z), 0.0) for z in totals])
        for k in range(8):
            put(buf, later, k, base, flow[k])

        @pl.when(tile == REACH + 1)
        def _():
            for k in range(8):
                held[0, k] = totals[k]

        return least

    least = lax.fori_loop(lo, hi, turn_step, one)
    for k in range(8):
        for tile in (1, 2, TILES - 1, TILES):
            put(buf, later, k, 8 * tile, zero)
        for tile in range(1, TILES + 1):
            put(buf, now, k, 8 * tile, zero)
    own = pl.ds(mine, 8)
    for k in range(8):
        values_ref[k] = (jnp.log(held[0, k, :, EDGE : EDGE + TC] * (1.0 / Z_SCALE)) - cost_ref[...]) / ITERS
    good = jnp.min(least) >= Z_FLOOR

    def forth_step(t, visits):
        now, later = (t + ITERS) & 1, 1 - ((t + ITERS) & 1)
        lo, hi = span(ITERS - 1 - t)

        def tile_step(tile, carry):
            base = pl.multiple_of(8 * tile, 8)
            e = damp[pl.ds(base, 8), :]
            flow = mix(forth, [shifted(buf, now, k, base, -1) * e for k in range(8)])
            for k in range(8):
                put(buf, later, k, base, flow[k])
            return carry

        lax.fori_loop(lo, hi, tile_step, 0)
        e = damp[own, :]
        total = zero
        for k in range(8):
            total = total + shifted(buf, now, k, mine, -1) * held[t + 1, k]
        return visits + total * e

    visits = lax.fori_loop(0, ITERS - 1, forth_step, zero)
    last = (2 * ITERS - 1) & 1
    total = zero
    for k in range(8):
        total = total + shifted(buf, last, k, mine, -1)
    block = mid_ref[pos]
    total = total * jnp.where(block[0:8] > 0.0, jnp.exp(block[8:16]) * Z_SCALE, 0.0)
    visits_ref[...] = (visits + total)[:, EDGE : EDGE + TC] * (1.0 / Y_SCALE)

    @pl.when(jnp.logical_not(good))
    def _():
        load_window(True)

        def log_total(h):
            most = picked[moves_ref[h, 0]]
            for a in range(1, 8):
                most = jnp.maximum(most, picked[moves_ref[h, a]])
            part = zero
            for a in range(8):
                part = part + jnp.exp(picked[moves_ref[h, a]] - most)
            return most + jnp.log(part)

        for tile in (0, TILES + 1):
            for k in range(8):
                for slot in range(2):
                    put(buf, slot, k, 8 * tile, zero)

        def slow_back(n, carry):
            t = ITERS - 1 - n
            now, later = n & 1, 1 - (n & 1)

            def keep(tile, carry):
                base = pl.multiple_of(8 * tile, 8)
                for k in range(8):
                    put(stack, n, k, pl.multiple_of(base - 16, 8), take(buf, now, k, base))
                return carry

            lax.fori_loop(2, TILES, keep, 0)
            lo, hi = span(t + 20)

            def tile_step(tile, carry):
                base = pl.multiple_of(8 * tile, 8)
                for k in range(8):
                    picked[k] = shifted(buf, now, k, base, 1)
                enter = damp[pl.ds(base, 8), :]

                def heading(h, carry):
                    total = log_total(h)
                    put(buf, later, h, base, jnp.where(enter > 0.0, total - enter, 0.0))

                    @pl.when((t == 0) & (tile == REACH + 1))
                    def _():
                        values_ref[h] = (total[:, EDGE : EDGE + TC] - cost_ref[...]) / ITERS

                    return carry

                return lax.fori_loop(0, 8, heading, carry)

            return lax.fori_loop(lo, hi, tile_step, carry)

        lax.fori_loop(0, ITERS, slow_back, 0)
        for slot in range(2):
            for k in range(8):
                for tile in range(TILES + 2):
                    put(buf, slot, k, 8 * tile, zero)

        def slow_forth(t, visits):
            now, later = t & 1, 1 - (t & 1)
            lo, hi = span(ITERS - t)

            def tile_step(tile, carry):
                base = pl.multiple_of(8 * tile, 8)
                inside = damp[pl.ds(base, 8), :] > 0.0
                mass = start[pl.ds(base, 8), :]
                for k in range(8):
                    picked[k] = shifted(stack, ITERS - 1 - t, k, pl.multiple_of(base - 16, 8), 1)
                    gathered[k] = zero
                    come = jnp.where(inside, shifted(buf, now, k, base, -1), 0.0)
                    gathered[8 + k] = jnp.where(t == 0, mass, come)

                def heading(h, carry):
                    total = log_total(h)
                    here = gathered[8 + h]
                    for a in range(8):
                        k = moves_ref[h, a]
                        gathered[k] = gathered[k] + here * jnp.exp(picked[k] - total)
                    return carry

                lax.fori_loop(0, 8, heading, 0)
                for k in range(8):
                    put(buf, later, k, base, gathered[k])
                return carry

            lax.fori_loop(lo, hi, tile_step, 0)
            total = zero
            for k in range(8):
                total = total + shifted(buf, later, k, mine, -1)
            return visits + total

        visits = lax.fori_loop(0, ITERS, slow_forth, zero)
        visits_ref[...] = visits[:, EDGE : EDGE + TC]


def window_call(pos, move_table, up, mid, down, cell_cost):
    smem = pl.BlockSpec(memory_space=pltpu.SMEM)
    vmem = pl.BlockSpec(memory_space=pltpu.VMEM)
    rows = 8 * (TILES + 2)
    return pl.pallas_call(
        main_kernel,
        in_specs=[smem, vmem, smem, vmem, vmem, vmem, vmem],
        out_specs=[vmem, vmem],
        out_shape=[
            jax.ShapeDtypeStruct((8, TR, TC), jnp.float32),
            jax.ShapeDtypeStruct((TR, TC), jnp.float32),
        ],
        scratch_shapes=[
            pltpu.VMEM((rows, WIDE), jnp.float32),
            pltpu.VMEM((rows, WIDE), jnp.float32),
            pltpu.VMEM((rows, WIDE), jnp.float32),
            pltpu.VMEM((2, 8, LANES, rows, 128), jnp.float32),
            pltpu.VMEM((ITERS, 8, 8, WIDE), jnp.float32),
            pltpu.VMEM((ITERS, 8, LANES, 72, 128), jnp.float32),
            pltpu.VMEM((8, 8, WIDE), jnp.float32),
            pltpu.VMEM((16, 8, WIDE), jnp.float32),
        ],
        compiler_params=pltpu.CompilerParams(vmem_limit_bytes=50 * 2**20),
        name="raster_steps",
    )(pos, move_table, move_table, up, mid, down, cell_cost)


def prepare_call(cell_cost, blocked, cells, mass):
    return pl.pallas_call(
        prepare_kernel,
        out_shape=jax.ShapeDtypeStruct((24, TC), jnp.float32),
        name="raster_prepare",
    )(cell_cost, blocked, cells, mass)


def on_device(cell_cost, blocked, move_table, anchor_cells, anchor_mass):
    n_rows, n_cols = lax.axis_size("rows"), lax.axis_size("cols")
    own = prepare_call(cell_cost, blocked, anchor_cells.reshape(1, 128), anchor_mass.reshape(1, 128))
    left = lax.ppermute(own[:, TC - EDGE :], "cols", [(i, i + 1) for i in range(n_cols - 1)])
    right = lax.ppermute(own[:, :EDGE], "cols", [(i + 1, i) for i in range(n_cols - 1)])
    strip = jnp.concatenate([left, own, right], axis=1)
    groups = [list(range(g, g + GROUP)) for g in range(0, n_rows, GROUP)]
    mid = lax.all_gather(strip, "rows", axis_index_groups=groups)
    up = lax.ppermute(mid[GROUP - REACH :], "rows", [(i, i + GROUP) for i in range(n_rows - GROUP)])
    down = lax.ppermute(mid[:REACH], "rows", [(i + GROUP, i) for i in range(n_rows - GROUP)])
    pos = lax.rem(lax.axis_index("rows"), GROUP).astype(jnp.int32).reshape(1)
    values, visits = window_call(pos, move_table, up, mid, down, cell_cost)
    return values, visits


def solution(mesh):
    placed = (
        P("rows", "cols"),
        P("rows", "cols"),
        P(),
        P("rows", "cols", None),
        P("rows", "cols", None),
    )
    return jax.shard_map(
        on_device,
        mesh=mesh,
        in_specs=placed,
        out_specs=(P(None, "rows", "cols"), P("rows", "cols")),
        check_vma=False,
    )
```

```python
import functools

import jax
import jax.numpy as jnp
from jax import lax
from jax.experimental import pallas as pl
from jax.experimental.pallas import tpu as pltpu
from jax.sharding import PartitionSpec as P

ITERS = 20
PENALTY = 3.0
ROW_STEP = (0, -1, -1, -1, 0, 1, 1, 1)
COL_STEP = (1, 1, 0, -1, -1, -1, 0, 1)
TR, TC = 8, 512
REACH = 5
EDGE = 64
WIDE = TC + 2 * EDGE
LANES = WIDE // 128
TILES = 2 * REACH + 1
GROUP = 8
Z_SCALE = 2.0**60
Y_SCALE = 2.0**30
Z_FLOOR = 2.0**-36


def prepare_kernel(cost_ref, blocked_ref, cells_ref, mass_ref, out_ref):
    penalty = -PENALTY * blocked_ref[...].astype(jnp.float32)
    out_ref[0:8] = cost_ref[...] - penalty
    out_ref[8:16] = penalty
    cells = cells_ref[...]
    row = lax.broadcasted_iota(jnp.int32, (TR, 128), 0)
    weight = jnp.where(row == (cells >> 9), mass_ref[...], 0.0)
    col = lax.broadcasted_iota(jnp.int32, (TC, 128), 0)
    hot = jnp.where(col == (cells & (TC - 1)), 1.0, 0.0)
    start = lax.dot_general(
        weight, hot, (((1,), (1,)), ((), ())),
        preferred_element_type=jnp.float32, precision=lax.Precision.HIGHEST,
    )
    out_ref[16:24] = start * 0.125


def take(buf, k, base):
    return jnp.concatenate([buf[k, l, pl.ds(base, 8), :] for l in range(LANES)], axis=1)


def put(buf, k, base, x):
    for l in range(LANES):
        buf[k, l, pl.ds(base, 8), :] = x[:, 128 * l : 128 * l + 128]


def shifted(buf, k, base, sign):
    dr, dc = sign * ROW_STEP[k], sign * COL_STEP[k]
    x = take(buf, k, base + dr)
    return pltpu.roll(x, (-dc) % WIDE, 1) if dc else x


def mix(mat, tiles):
    x = jnp.concatenate([jnp.concatenate([p[k] for p in tiles], axis=1) for k in range(8)], axis=0)
    hi = x.astype(jnp.bfloat16)
    lo = (x - hi.astype(jnp.float32)).astype(jnp.bfloat16)
    y = jnp.dot(mat, jnp.concatenate([hi, lo], axis=0), preferred_element_type=jnp.float32)
    return [[y[8 * k : 8 * k + 8, WIDE * u : WIDE * (u + 1)] for k in range(8)] for u in range(len(tiles))]


def reach(radius):
    return (radius + 7) // 8


def span(radius):
    far = (radius + 7) // 8
    return REACH - far + 1, REACH + far + 2


def main_kernel(
    pos_ref, table_ref, moves_ref, up_ref, mid_ref, down_ref, cost_ref, values_ref, visits_ref,
    damp, outer, start, even, odd, held, lowest, total_visits, stack, picked, gathered,
):
    pos = pos_ref[0]
    lane = lax.broadcasted_iota(jnp.int32, (8, WIDE), 1)
    sub = lax.broadcasted_iota(jnp.int32, (8, WIDE), 0)
    zero = jnp.zeros((8, WIDE), jnp.float32)
    one = jnp.full((8, WIDE), Z_SCALE, jnp.float32)
    for k in range(8):
        for edge in (0, TILES + 1):
            put(even, k, 8 * edge, one)
            put(odd, k, 8 * edge, one)

    def fetch(src, at, tile, raw):
        block = src[at]
        enter, pen, mass = block[0:8], block[8:16], block[16:24]
        base = pl.multiple_of(8 * tile, 8)
        inside = enter > 0.0
        row = 8 * tile + sub - 8 * (REACH + 1)
        near = (row >= -20) & (row < TR + 20) & (lane >= EDGE - 20) & (lane < EDGE + TC + 20)
        start[pl.ds(base, 8), :] = jnp.where(near, mass, 0.0)
        if raw:
            damp[pl.ds(base, 8), :] = enter
            first = pen
        else:
            damp[pl.ds(base, 8), :] = jnp.where(inside, jnp.exp(-enter), 0.0)
            outer[pl.ds(base, 8), :] = jnp.where(inside, 0.0, one)
            first = jnp.exp(pen) * Z_SCALE
        for k in range(8):
            put(even, k, base, first)

    def load_window(raw):
        def body(tile, carry):
            at = pos + tile - 1

            @pl.when(at < REACH)
            def _():
                fetch(up_ref, at, tile, raw)

            @pl.when((at >= REACH) & (at < REACH + GROUP))
            def _():
                fetch(mid_ref, at - REACH, tile, raw)

            @pl.when(at >= REACH + GROUP)
            def _():
                fetch(down_ref, at - REACH - GROUP, tile, raw)

            return carry

        lax.fori_loop(1, TILES + 1, body, 0)

    load_window(False)

    table = jnp.broadcast_to(table_ref[...].reshape(8, 1, 8), (8, 8, 8)).reshape(64, 8)
    col = lax.broadcasted_iota(jnp.int32, (64, 64), 1)
    row = lax.broadcasted_iota(jnp.int32, (64, 64), 0)
    count = jnp.zeros((64, 64), jnp.float32)
    for a in range(8):
        count = count + jnp.where(table[:, a : a + 1] == (col >> 3), 1.0, 0.0)
    count = jnp.where((row & 7) == (col & 7), count, 0.0)
    back = jnp.concatenate([count, count], axis=1).astype(jnp.bfloat16)
    turned = count.T
    forth = jnp.concatenate([turned, turned], axis=1).astype(jnp.bfloat16)
    mine = 8 * (REACH + 1)

    center = REACH + 1

    def over_tiles(far, work):
        work([8 * (center - 1), 8 * center, 8 * (center + 1)])

        def pair(j, carry):
            work([pl.multiple_of(8 * (center - j), 8), pl.multiple_of(8 * (center + j), 8)])
            return carry

        lax.fori_loop(2, far + 1, pair, 0)

    def back_step(t, now, later):
        def work(bases):
            totals = mix(back, [[shifted(now, k, b, 1) for k in range(8)] for b in bases])
            for b, total in zip(bases, totals):
                e, o = damp[pl.ds(b, 8), :], outer[pl.ds(b, 8), :]
                for k in range(8):
                    z = total[k] * e + o
                    put(later, k, b, z)
                    if len(bases) == 3 and b is bases[1]:
                        held[t, k] = z

        over_tiles(reach(t + 20), work)

    def back_pair(n, carry):
        back_step(ITERS - 1 - 2 * n, even, odd)
        back_step(ITERS - 2 - 2 * n, odd, even)
        return carry

    for k in range(8):
        held[ITERS, k] = take(even, k, mine)
    lax.fori_loop(0, ITERS // 2 - 1, back_pair, 0)
    back_step(1, even, odd)
    lowest[...] = one

    def turn(bases):
        totals = mix(back, [[shifted(odd, k, b, 1) for k in range(8)] for b in bases])
        share = []
        for b, total in zip(bases, totals):
            row = b + sub - mine
            near = (row >= -20) & (row < TR + 20) & (lane >= EDGE - 20) & (lane < EDGE + TC + 20)
            live = near & (damp[pl.ds(b, 8), :] > 0.0)
            low = total[0]
            for k in range(1, 8):
                low = jnp.minimum(low, total[k])
            lowest[...] = jnp.minimum(lowest[...], jnp.where(live, low, Z_SCALE))
            mass = start[pl.ds(b, 8), :] * Y_SCALE
            live = live & (mass > 0.0)
            share.append([jnp.where(live, mass / z, 0.0) for z in total])
            if len(bases) == 3 and b is bases[1]:
                for k in range(8):
                    z = total[k][:, EDGE : EDGE + TC] * (1.0 / Z_SCALE)
                    values_ref[k] = (jnp.log(z) - cost_ref[...]) / ITERS
        flows = mix(forth, share)
        for b, flow in zip(bases, flows):
            for k in range(8):
                put(even, k, b, flow[k])

    over_tiles(reach(20), turn)
    for k in range(8):
        for tile in (center - 4, center + 4):
            put(even, k, 8 * tile, zero)
            put(odd, k, 8 * tile, zero)
    good = jnp.min(lowest[...]) >= Z_FLOOR

    total_visits[...] = zero

    def forth_step(t, now, later):
        def work(bases):
            arrive = [[shifted(now, k, b, -1) for k in range(8)] for b in bases]
            if len(bases) == 3:
                total = total_visits[...]
                for k in range(8):
                    total = total + arrive[1][k] * held[t + 1, k]
                total_visits[...] = total
            damps = [damp[pl.ds(b, 8), :] for b in bases]
            flows = mix(forth, [[x * e for x in part] for e, part in zip(damps, arrive)])
            for b, flow in zip(bases, flows):
                for k in range(8):
                    put(later, k, b, flow[k])

        over_tiles(reach(ITERS - 1 - t), work)

    def forth_pair(n, carry):
        forth_step(2 * n, even, odd)
        forth_step(2 * n + 1, odd, even)
        return carry

    lax.fori_loop(0, ITERS // 2 - 1, forth_pair, 0)
    forth_step(ITERS - 2, even, odd)
    total = total_visits[...]
    for k in range(8):
        total = total + shifted(odd, k, mine, -1) * held[ITERS, k]
    visits_ref[...] = total[:, EDGE : EDGE + TC] * (1.0 / Y_SCALE)

    @pl.when(jnp.logical_not(good))
    def _():
        load_window(True)

        def log_total(h):
            most = picked[moves_ref[h, 0]]
            for a in range(1, 8):
                most = jnp.maximum(most, picked[moves_ref[h, a]])
            part = zero
            for a in range(8):
                part = part + jnp.exp(picked[moves_ref[h, a]] - most)
            return most + jnp.log(part)

        for tile in (0, TILES + 1):
            for k in range(8):
                put(even, k, 8 * tile, zero)

        def settle():
            def body(tile, carry):
                base = pl.multiple_of(8 * tile, 8)
                for k in range(8):
                    put(even, k, base, take(odd, k, base))
                return carry

            lax.fori_loop(1, TILES + 1, body, 0)

        def slow_back(n, carry):
            t = ITERS - 1 - n

            def keep(tile, carry):
                base = pl.multiple_of(8 * tile, 8)
                for k in range(8):
                    put(stack.at[n], k, pl.multiple_of(base - 16, 8), take(even, k, base))
                return carry

            lax.fori_loop(2, TILES, keep, 0)
            far = reach(t + 20)
            lo, hi = center - far, center + far + 1

            def tile_step(tile, carry):
                base = pl.multiple_of(8 * tile, 8)
                for k in range(8):
                    picked[k] = shifted(even, k, base, 1)
                enter = damp[pl.ds(base, 8), :]

                def heading(h, carry):
                    total = log_total(h)
                    put(odd, h, base, jnp.where(enter > 0.0, total - enter, 0.0))

                    @pl.when((t == 0) & (tile == REACH + 1))
                    def _():
                        values_ref[h] = (total[:, EDGE : EDGE + TC] - cost_ref[...]) / ITERS

                    return carry

                return lax.fori_loop(0, 8, heading, carry)

            lax.fori_loop(lo, hi, tile_step, 0)
            settle()
            return carry

        lax.fori_loop(0, ITERS, slow_back, 0)
        for k in range(8):
            for tile in range(TILES + 2):
                put(even, k, 8 * tile, zero)
                put(odd, k, 8 * tile, zero)

        def slow_forth(t, visits):
            far = reach(ITERS - t)
            lo, hi = center - far, center + far + 1

            def tile_step(tile, carry):
                base = pl.multiple_of(8 * tile, 8)
                inside = damp[pl.ds(base, 8), :] > 0.0
                mass = start[pl.ds(base, 8), :]
                for k in range(8):
                    picked[k] = shifted(stack.at[ITERS - 1 - t], k, pl.multiple_of(base - 16, 8), 1)
                    gathered[k] = zero
                    come = jnp.where(inside, shifted(even, k, base, -1), 0.0)
                    gathered[8 + k] = jnp.where(t == 0, mass, come)

                def heading(h, carry):
                    total = log_total(h)
                    here = gathered[8 + h]
                    for a in range(8):
                        k = moves_ref[h, a]
                        gathered[k] = gathered[k] + here * jnp.exp(picked[k] - total)
                    return carry

                lax.fori_loop(0, 8, heading, 0)
                for k in range(8):
                    put(odd, k, base, gathered[k])
                return carry

            lax.fori_loop(lo, hi, tile_step, 0)
            settle()
            total = zero
            for k in range(8):
                total = total + shifted(even, k, mine, -1)
            return visits + total

        visits = lax.fori_loop(0, ITERS, slow_forth, zero)
        visits_ref[...] = visits[:, EDGE : EDGE + TC]


def window_call(pos, move_table, up, mid, down, cell_cost):
    smem = pl.BlockSpec(memory_space=pltpu.SMEM)
    vmem = pl.BlockSpec(memory_space=pltpu.VMEM)
    rows = 8 * (TILES + 2)
    return pl.pallas_call(
        main_kernel,
        in_specs=[smem, vmem, smem, vmem, vmem, vmem, vmem],
        out_specs=[vmem, vmem],
        out_shape=[
            jax.ShapeDtypeStruct((8, TR, TC), jnp.float32),
            jax.ShapeDtypeStruct((TR, TC), jnp.float32),
        ],
        scratch_shapes=[
            pltpu.VMEM((rows, WIDE), jnp.float32),
            pltpu.VMEM((rows, WIDE), jnp.float32),
            pltpu.VMEM((rows, WIDE), jnp.float32),
            pltpu.VMEM((8, LANES, rows, 128), jnp.float32),
            pltpu.VMEM((8, LANES, rows, 128), jnp.float32),
            pltpu.VMEM((ITERS + 1, 8, 8, WIDE), jnp.float32),
            pltpu.VMEM((8, WIDE), jnp.float32),
            pltpu.VMEM((8, WIDE), jnp.float32),
            pltpu.VMEM((ITERS, 8, LANES, 72, 128), jnp.float32),
            pltpu.VMEM((8, 8, WIDE), jnp.float32),
            pltpu.VMEM((16, 8, WIDE), jnp.float32),
        ],
        compiler_params=pltpu.CompilerParams(vmem_limit_bytes=50 * 2**20),
        name="raster_steps",
    )(pos, move_table, move_table, up, mid, down, cell_cost)


def prepare_call(cell_cost, blocked, cells, mass):
    return pl.pallas_call(
        prepare_kernel,
        out_shape=jax.ShapeDtypeStruct((24, TC), jnp.float32),
        name="raster_prepare",
    )(cell_cost, blocked, cells, mass)


def on_device(cell_cost, blocked, move_table, anchor_cells, anchor_mass):
    n_rows, n_cols = lax.axis_size("rows"), lax.axis_size("cols")
    own = prepare_call(cell_cost, blocked, anchor_cells.reshape(1, 128), anchor_mass.reshape(1, 128))
    left = lax.ppermute(own[:, TC - EDGE :], "cols", [(i, i + 1) for i in range(n_cols - 1)])
    right = lax.ppermute(own[:, :EDGE], "cols", [(i + 1, i) for i in range(n_cols - 1)])
    strip = jnp.concatenate([left, own, right], axis=1)
    groups = [list(range(g, g + GROUP)) for g in range(0, n_rows, GROUP)]
    mid = lax.all_gather(strip, "rows", axis_index_groups=groups)
    up = lax.ppermute(mid[GROUP - REACH :], "rows", [(i, i + GROUP) for i in range(n_rows - GROUP)])
    down = lax.ppermute(mid[:REACH], "rows", [(i + GROUP, i) for i in range(n_rows - GROUP)])
    pos = lax.rem(lax.axis_index("rows"), GROUP).astype(jnp.int32).reshape(1)
    values, visits = window_call(pos, move_table, up, mid, down, cell_cost)
    return values, visits


def solution(mesh):
    placed = (
        P("rows", "cols"),
        P("rows", "cols"),
        P(),
        P("rows", "cols", None),
        P("rows", "cols", None),
    )
    return jax.shard_map(
        on_device,
        mesh=mesh,
        in_specs=placed,
        out_specs=(P(None, "rows", "cols"), P("rows", "cols")),
        check_vma=False,
    )
```

```python
import functools

import jax
import jax.numpy as jnp
from jax import lax
from jax.experimental import pallas as pl
from jax.experimental.pallas import tpu as pltpu
from jax.sharding import PartitionSpec as P

ITERS = 20
PENALTY = 3.0
ROW_STEP = (0, -1, -1, -1, 0, 1, 1, 1)
COL_STEP = (1, 1, 0, -1, -1, -1, 0, 1)
TR, TC = 8, 512
REACH = 5
EDGE = 64
WIDE = TC + 2 * EDGE
LANES = WIDE // 128
TILES = 2 * REACH + 1
GROUP = 8
CHUNK = 2
Z_SCALE = 2.0**60
Y_SCALE = 2.0**30
Z_FLOOR = 2.0**-36


def prepare_kernel(cost_ref, blocked_ref, cells_ref, mass_ref, out_ref):
    penalty = -PENALTY * blocked_ref[...].astype(jnp.float32)
    out_ref[0:8] = cost_ref[...] - penalty
    out_ref[8:16] = penalty
    cells = cells_ref[...]
    row = lax.broadcasted_iota(jnp.int32, (TR, 128), 0)
    weight = jnp.where(row == (cells >> 9), mass_ref[...], 0.0)
    col = lax.broadcasted_iota(jnp.int32, (TC, 128), 0)
    hot = jnp.where(col == (cells & (TC - 1)), 1.0, 0.0)
    start = lax.dot_general(
        weight, hot, (((1,), (1,)), ((), ())),
        preferred_element_type=jnp.float32, precision=lax.Precision.HIGHEST,
    )
    out_ref[16:24] = start * 0.125


def column_of(place):
    return LANES * (place & 127) + (place >> 7)


def moved(x, hot):
    first = x.astype(jnp.bfloat16)
    rest = x - first.astype(jnp.float32)
    second = rest.astype(jnp.bfloat16)
    third = (rest - second.astype(jnp.float32)).astype(jnp.bfloat16)
    n = x.shape[0]
    y = jnp.dot(jnp.concatenate([first, second, third], axis=0), hot, preferred_element_type=jnp.float32)
    return y[:n] + (y[n : 2 * n] + y[2 * n :])


def strip_kernel(left_ref, own_ref, right_ref, out_ref):
    x = jnp.concatenate([left_ref[...], own_ref[...], right_ref[...]], axis=1)
    column = lax.broadcasted_iota(jnp.int32, (WIDE, WIDE), 0)
    place = lax.broadcasted_iota(jnp.int32, (WIDE, WIDE), 1)
    hot = jnp.where(column == column_of(place), 1.0, 0.0).astype(jnp.bfloat16)
    out_ref[...] = moved(x, hot)


def take(buf, k, base):
    return jnp.concatenate([buf[k, l, pl.ds(base, 8), :] for l in range(LANES)], axis=1)


def put(buf, k, base, x):
    for l in range(LANES):
        buf[k, l, pl.ds(base, 8), :] = x[:, 128 * l : 128 * l + 128]


def shifted(buf, k, base, sign):
    dr, dc = sign * ROW_STEP[k], sign * COL_STEP[k]
    x = [buf[k, l, pl.ds(base + dr, 8), :] for l in range(LANES)]
    if dc == 1:
        x = x[1:] + [pltpu.roll(x[0], 127, 1)]
    if dc == -1:
        x = [pltpu.roll(x[-1], 1, 1)] + x[:-1]
    return jnp.concatenate(x, axis=1)


def mix(mat, tiles):
    x = jnp.concatenate([jnp.concatenate([p[k] for p in tiles], axis=1) for k in range(8)], axis=0)
    hi = x.astype(jnp.bfloat16)
    lo = (x - hi.astype(jnp.float32)).astype(jnp.bfloat16)
    y = jnp.dot(mat, jnp.concatenate([hi, lo], axis=0), preferred_element_type=jnp.float32)
    return [[y[8 * k : 8 * k + 8, WIDE * u : WIDE * (u + 1)] for k in range(8)] for u in range(len(tiles))]


def reach(radius):
    return (radius + 7) // 8


def span(radius):
    far = (radius + 7) // 8
    return REACH - far + 1, REACH + far + 2


def main_kernel(
    pos_ref, table_ref, moves_ref, up_ref, mid_ref, down_ref, cost_ref, values_ref, visits_ref,
    damp, outer, start, even, odd, held, lowest, total_visits, final, stack, picked, gathered,
):
    pos = pos_ref[0]
    lane = column_of(lax.broadcasted_iota(jnp.int32, (8, WIDE), 1))
    sub = lax.broadcasted_iota(jnp.int32, (8, WIDE), 0)
    zero = jnp.zeros((8, WIDE), jnp.float32)
    one = jnp.full((8, WIDE), Z_SCALE, jnp.float32)
    for k in range(8):
        for edge in (0, TILES + 1):
            put(even, k, 8 * edge, one)
            put(odd, k, 8 * edge, one)

    def fetch(src, at, tile, raw):
        block = src[at]
        enter, pen, mass = block[0:8], block[8:16], block[16:24]
        base = pl.multiple_of(8 * tile, 8)
        inside = enter > 0.0
        row = 8 * tile + sub - 8 * (REACH + 1)
        near = (row >= -20) & (row < TR + 20) & (lane >= EDGE - 20) & (lane < EDGE + TC + 20)
        start[pl.ds(base, 8), :] = jnp.where(near, mass, 0.0)
        if raw:
            damp[pl.ds(base, 8), :] = enter
            first = pen
        else:
            damp[pl.ds(base, 8), :] = jnp.where(inside, jnp.exp(-enter), 0.0)
            outer[pl.ds(base, 8), :] = jnp.where(inside, 0.0, one)
            first = jnp.exp(pen) * Z_SCALE
        for k in range(8):
            put(even, k, base, first)

    def load_window(raw):
        def body(tile, carry):
            at = pos + tile - 1

            @pl.when(at < REACH)
            def _():
                fetch(up_ref, at, tile, raw)

            @pl.when((at >= REACH) & (at < REACH + GROUP))
            def _():
                fetch(mid_ref, at - REACH, tile, raw)

            @pl.when(at >= REACH + GROUP)
            def _():
                fetch(down_ref, at - REACH - GROUP, tile, raw)

            return carry

        lax.fori_loop(1, TILES + 1, body, 0)

    load_window(False)

    table = jnp.broadcast_to(table_ref[...].reshape(8, 1, 8), (8, 8, 8)).reshape(64, 8)
    col = lax.broadcasted_iota(jnp.int32, (64, 64), 1)
    row = lax.broadcasted_iota(jnp.int32, (64, 64), 0)
    count = jnp.zeros((64, 64), jnp.float32)
    for a in range(8):
        count = count + jnp.where(table[:, a : a + 1] == (col >> 3), 1.0, 0.0)
    count = jnp.where((row & 7) == (col & 7), count, 0.0)
    back = jnp.concatenate([count, count], axis=1).astype(jnp.bfloat16)
    turned = count.T
    forth = jnp.concatenate([turned, turned], axis=1).astype(jnp.bfloat16)
    mine = 8 * (REACH + 1)

    center = REACH + 1

    def over_tiles(far, work):
        tiles = list(range(center - far, center + far + 1))
        for first in range(0, len(tiles), CHUNK):
            work([8 * tile for tile in tiles[first : first + CHUNK]])

    def in_pairs(first, last, sources, far, step):
        def turn(n, carry):
            step(first + 2 * n, sources[0], sources[1], far)
            step(first + 2 * n + 1, sources[1], sources[0], far)
            return carry

        lax.fori_loop(0, (last - first) // 2, turn, 0)

    def back_step(n, now, later, far):
        t = ITERS - 1 - n

        def work(bases):
            totals = mix(back, [[shifted(now, k, b, 1) for k in range(8)] for b in bases])
            for b, total in zip(bases, totals):
                e, o = damp[pl.ds(b, 8), :], outer[pl.ds(b, 8), :]
                for k in range(8):
                    z = total[k] * e + o
                    put(later, k, b, z)
                    if b == mine:
                        held[t, k] = z

        over_tiles(far, work)

    for k in range(8):
        held[ITERS, k] = take(even, k, mine)
    in_pairs(0, 8, (even, odd), 5, back_step)
    in_pairs(8, 16, (even, odd), 4, back_step)
    in_pairs(16, 18, (even, odd), 3, back_step)
    back_step(18, even, odd, 3)
    lowest[...] = one

    def turn(bases):
        totals = mix(back, [[shifted(odd, k, b, 1) for k in range(8)] for b in bases])
        share = []
        for b, total in zip(bases, totals):
            row = b + sub - mine
            near = (row >= -20) & (row < TR + 20) & (lane >= EDGE - 20) & (lane < EDGE + TC + 20)
            live = near & (damp[pl.ds(b, 8), :] > 0.0)
            low = total[0]
            for k in range(1, 8):
                low = jnp.minimum(low, total[k])
            lowest[...] = jnp.minimum(lowest[...], jnp.where(live, low, Z_SCALE))
            mass = start[pl.ds(b, 8), :] * Y_SCALE
            live = live & (mass > 0.0)
            share.append([jnp.where(live, mass / z, 0.0) for z in total])
            if b == mine:
                for k in range(8):
                    final[8 * k : 8 * k + 8, :] = jnp.log(total[k] * (1.0 / Z_SCALE))
        flows = mix(forth, share)
        for b, flow in zip(bases, flows):
            for k in range(8):
                put(even, k, b, flow[k])

    over_tiles(3, turn)
    for k in range(8):
        for tile in (center - 4, center + 4):
            put(even, k, 8 * tile, zero)
            put(odd, k, 8 * tile, zero)
    good = jnp.min(lowest[...]) >= Z_FLOOR

    total_visits[...] = zero

    def forth_step(t, now, later, far):
        def work(bases):
            arrive = [[shifted(now, k, b, -1) for k in range(8)] for b in bases]
            if mine in bases:
                total = total_visits[...]
                for k in range(8):
                    total = total + arrive[bases.index(mine)][k] * held[t + 1, k]
                total_visits[...] = total
            damps = [damp[pl.ds(b, 8), :] for b in bases]
            flows = mix(forth, [[x * e for x in part] for e, part in zip(damps, arrive)])
            for b, flow in zip(bases, flows):
                for k in range(8):
                    put(later, k, b, flow[k])

        over_tiles(far, work)

    in_pairs(0, 4, (even, odd), 3, forth_step)
    in_pairs(4, 12, (even, odd), 2, forth_step)
    in_pairs(12, 18, (even, odd), 1, forth_step)
    forth_step(18, even, odd, 1)
    total = total_visits[...]
    for k in range(8):
        total = total + shifted(odd, k, mine, -1) * held[ITERS, k]
    final[64:72, :] = total * (1.0 / Y_SCALE)

    @pl.when(jnp.logical_not(good))
    def _():
        load_window(True)

        def log_total(h):
            most = picked[moves_ref[h, 0]]
            for a in range(1, 8):
                most = jnp.maximum(most, picked[moves_ref[h, a]])
            part = zero
            for a in range(8):
                part = part + jnp.exp(picked[moves_ref[h, a]] - most)
            return most + jnp.log(part)

        for tile in (0, TILES + 1):
            for k in range(8):
                put(even, k, 8 * tile, zero)

        def settle():
            def body(tile, carry):
                base = pl.multiple_of(8 * tile, 8)
                for k in range(8):
                    put(even, k, base, take(odd, k, base))
                return carry

            lax.fori_loop(1, TILES + 1, body, 0)

        def slow_back(n, carry):
            t = ITERS - 1 - n

            def keep(tile, carry):
                base = pl.multiple_of(8 * tile, 8)
                for k in range(8):
                    put(stack.at[n], k, pl.multiple_of(base - 16, 8), take(even, k, base))
                return carry

            lax.fori_loop(2, TILES, keep, 0)
            far = reach(t + 20)
            lo, hi = center - far, center + far + 1

            def tile_step(tile, carry):
                base = pl.multiple_of(8 * tile, 8)
                for k in range(8):
                    picked[k] = shifted(even, k, base, 1)
                enter = damp[pl.ds(base, 8), :]

                def heading(h, carry):
                    total = log_total(h)
                    put(odd, h, base, jnp.where(enter > 0.0, total - enter, 0.0))

                    @pl.when((t == 0) & (tile == REACH + 1))
                    def _():
                        final[pl.ds(pl.multiple_of(8 * h, 8), 8), :] = total

                    return carry

                return lax.fori_loop(0, 8, heading, carry)

            lax.fori_loop(lo, hi, tile_step, 0)
            settle()
            return carry

        lax.fori_loop(0, ITERS, slow_back, 0)
        for k in range(8):
            for tile in range(TILES + 2):
                put(even, k, 8 * tile, zero)
                put(odd, k, 8 * tile, zero)

        def slow_forth(t, visits):
            far = reach(ITERS - t)
            lo, hi = center - far, center + far + 1

            def tile_step(tile, carry):
                base = pl.multiple_of(8 * tile, 8)
                inside = damp[pl.ds(base, 8), :] > 0.0
                mass = start[pl.ds(base, 8), :]
                for k in range(8):
                    picked[k] = shifted(stack.at[ITERS - 1 - t], k, pl.multiple_of(base - 16, 8), 1)
                    gathered[k] = zero
                    come = jnp.where(inside, shifted(even, k, base, -1), 0.0)
                    gathered[8 + k] = jnp.where(t == 0, mass, come)

                def heading(h, carry):
                    total = log_total(h)
                    here = gathered[8 + h]
                    for a in range(8):
                        k = moves_ref[h, a]
                        gathered[k] = gathered[k] + here * jnp.exp(picked[k] - total)
                    return carry

                lax.fori_loop(0, 8, heading, 0)
                for k in range(8):
                    put(odd, k, base, gathered[k])
                return carry

            lax.fori_loop(lo, hi, tile_step, 0)
            settle()
            total = zero
            for k in range(8):
                total = total + shifted(even, k, mine, -1)
            return visits + total

        visits = lax.fori_loop(0, ITERS, slow_forth, zero)
        final[64:72, :] = visits

    place = lax.broadcasted_iota(jnp.int32, (WIDE, TC), 0)
    column = lax.broadcasted_iota(jnp.int32, (WIDE, TC), 1)
    hot = jnp.where(column_of(place) == column + EDGE, 1.0, 0.0).astype(jnp.bfloat16)
    out = moved(final[...], hot)
    for k in range(8):
        values_ref[k] = (out[8 * k : 8 * k + 8] - cost_ref[...]) / ITERS
    visits_ref[...] = out[64:72]


def window_call(pos, move_table, up, mid, down, cell_cost):
    smem = pl.BlockSpec(memory_space=pltpu.SMEM)
    vmem = pl.BlockSpec(memory_space=pltpu.VMEM)
    rows = 8 * (TILES + 2)
    return pl.pallas_call(
        main_kernel,
        in_specs=[smem, vmem, smem, vmem, vmem, vmem, vmem],
        out_specs=[vmem, vmem],
        out_shape=[
            jax.ShapeDtypeStruct((8, TR, TC), jnp.float32),
            jax.ShapeDtypeStruct((TR, TC), jnp.float32),
        ],
        scratch_shapes=[
            pltpu.VMEM((rows, WIDE), jnp.float32),
            pltpu.VMEM((rows, WIDE), jnp.float32),
            pltpu.VMEM((rows, WIDE), jnp.float32),
            pltpu.VMEM((8, LANES, rows, 128), jnp.float32),
            pltpu.VMEM((8, LANES, rows, 128), jnp.float32),
            pltpu.VMEM((ITERS + 1, 8, 8, WIDE), jnp.float32),
            pltpu.VMEM((8, WIDE), jnp.float32),
            pltpu.VMEM((8, WIDE), jnp.float32),
            pltpu.VMEM((72, WIDE), jnp.float32),
            pltpu.VMEM((ITERS, 8, LANES, 72, 128), jnp.float32),
            pltpu.VMEM((8, 8, WIDE), jnp.float32),
            pltpu.VMEM((16, 8, WIDE), jnp.float32),
        ],
        compiler_params=pltpu.CompilerParams(vmem_limit_bytes=50 * 2**20),
        name="raster_steps",
    )(pos, move_table, move_table, up, mid, down, cell_cost)


def prepare_call(cell_cost, blocked, cells, mass):
    return pl.pallas_call(
        prepare_kernel,
        out_shape=jax.ShapeDtypeStruct((24, TC), jnp.float32),
        name="raster_prepare",
    )(cell_cost, blocked, cells, mass)


def strip_call(left, own, right):
    return pl.pallas_call(
        strip_kernel,
        out_shape=jax.ShapeDtypeStruct((24, WIDE), jnp.float32),
        name="raster_strip",
    )(left, own, right)


def on_device(cell_cost, blocked, move_table, anchor_cells, anchor_mass):
    n_rows, n_cols = lax.axis_size("rows"), lax.axis_size("cols")
    own = prepare_call(cell_cost, blocked, anchor_cells.reshape(1, 128), anchor_mass.reshape(1, 128))
    left = lax.ppermute(own[:, TC - EDGE :], "cols", [(i, i + 1) for i in range(n_cols - 1)])
    right = lax.ppermute(own[:, :EDGE], "cols", [(i + 1, i) for i in range(n_cols - 1)])
    strip = strip_call(left, own, right)
    groups = [list(range(g, g + GROUP)) for g in range(0, n_rows, GROUP)]
    mid = lax.all_gather(strip, "rows", axis_index_groups=groups)
    up = lax.ppermute(mid[GROUP - REACH :], "rows", [(i, i + GROUP) for i in range(n_rows - GROUP)])
    down = lax.ppermute(mid[:REACH], "rows", [(i + GROUP, i) for i in range(n_rows - GROUP)])
    pos = lax.rem(lax.axis_index("rows"), GROUP).astype(jnp.int32).reshape(1)
    values, visits = window_call(pos, move_table, up, mid, down, cell_cost)
    return values, visits


def solution(mesh):
    placed = (
        P("rows", "cols"),
        P("rows", "cols"),
        P(),
        P("rows", "cols", None),
        P("rows", "cols", None),
    )
    return jax.shard_map(
        on_device,
        mesh=mesh,
        in_specs=placed,
        out_specs=(P(None, "rows", "cols"), P("rows", "cols")),
        check_vma=False,
    )
```

```python
import functools

import jax
import jax.numpy as jnp
from jax import lax
from jax.experimental import pallas as pl
from jax.experimental.pallas import tpu as pltpu
from jax.sharding import PartitionSpec as P

ITERS = 20
PENALTY = 3.0
ROW_STEP = (0, -1, -1, -1, 0, 1, 1, 1)
COL_STEP = (1, 1, 0, -1, -1, -1, 0, 1)
TR, TC = 8, 512
REACH = 5
EDGE = 64
WIDE = TC + 2 * EDGE
LANES = WIDE // 128
TILES = 2 * REACH + 1
GROUP = 8
CHUNK = 2
Z_SCALE = 2.0**60
Y_SCALE = 2.0**30
Z_FLOOR = 2.0**-36


def terms(x):
    first = x.astype(jnp.bfloat16)
    rest = x - first.astype(jnp.float32)
    second = rest.astype(jnp.bfloat16)
    third = (rest - second.astype(jnp.float32)).astype(jnp.bfloat16)
    return jnp.concatenate([first, second, third], axis=0)


def summed(y, n):
    return y[:n] + (y[n : 2 * n] + y[2 * n :])


def prepare_kernel(cost_ref, blocked_ref, cells_ref, mass_ref, own_ref, first_ref, last_ref):
    penalty = -PENALTY * blocked_ref[...].astype(jnp.float32)
    cells = cells_ref[...]
    row = lax.broadcasted_iota(jnp.int32, (TR, 128), 0)
    weight = jnp.where(row == (cells >> 9), mass_ref[...] * 0.125, 0.0)
    col = lax.broadcasted_iota(jnp.int32, (TC, 128), 0)
    hot = jnp.where(col == (cells & (TC - 1)), 1.0, 0.0).astype(jnp.bfloat16)
    start = summed(
        lax.dot_general(terms(weight), hot, (((1,), (1,)), ((), ())), preferred_element_type=jnp.float32), TR
    )
    own = jnp.concatenate([cost_ref[...] - penalty, penalty, start], axis=0)
    own_ref[...] = own
    first_ref[...] = own[:, :EDGE]
    last_ref[...] = own[:, TC - EDGE :]


def column_of(place):
    return LANES * (place & 127) + (place >> 7)


def moved(x, hot):
    return summed(jnp.dot(terms(x), hot, preferred_element_type=jnp.float32), x.shape[0])


def hot_matrix(columns, wide):
    place = lax.broadcasted_iota(jnp.int32, (columns.shape[0], wide), 1)
    return jnp.where(columns == column_of(place), 1.0, 0.0).astype(jnp.bfloat16)


def aside_kernel(own_ref, table_ref, out_ref, back_ref, forth_ref, hot_ref):
    column = lax.broadcasted_iota(jnp.int32, (TC, WIDE), 0) + EDGE
    out_ref[...] = moved(own_ref[...], hot_matrix(column, WIDE))
    table = jnp.broadcast_to(table_ref[...].reshape(8, 1, 8), (8, 8, 8)).reshape(64, 8)
    col = lax.broadcasted_iota(jnp.int32, (64, 64), 1)
    row = lax.broadcasted_iota(jnp.int32, (64, 64), 0)
    count = jnp.zeros((64, 64), jnp.float32)
    for a in range(8):
        count = count + jnp.where(table[:, a : a + 1] == (col >> 3), 1.0, 0.0)
    count = jnp.where((row & 7) == (col & 7), count, 0.0)
    turned = count.T
    back_ref[...] = jnp.concatenate([count, count], axis=1).astype(jnp.bfloat16)
    forth_ref[...] = jnp.concatenate([turned, turned], axis=1).astype(jnp.bfloat16)
    place = lax.broadcasted_iota(jnp.int32, (WIDE, TC), 0)
    column = lax.broadcasted_iota(jnp.int32, (WIDE, TC), 1) + EDGE
    hot_ref[...] = jnp.where(column_of(place) == column, 1.0, 0.0).astype(jnp.bfloat16)


def strip_kernel(left_ref, right_ref, own_ref, out_ref):
    x = jnp.concatenate([left_ref[...], right_ref[...]], axis=1)
    column = lax.broadcasted_iota(jnp.int32, (2 * EDGE, WIDE), 0)
    column = jnp.where(column < EDGE, column, column + TC)
    out_ref[...] = own_ref[...] + moved(x, hot_matrix(column, WIDE))


def take(buf, k, base):
    return jnp.concatenate([buf[k, l, pl.ds(base, 8), :] for l in range(LANES)], axis=1)


def put(buf, k, base, x):
    for l in range(LANES):
        buf[k, l, pl.ds(base, 8), :] = x[:, 128 * l : 128 * l + 128]


def put_inside(buf, k, base, x, inside):
    for l in range(LANES):
        part = slice(128 * l, 128 * l + 128)
        pltpu.store(buf.at[k, l, pl.ds(base, 8), :], x[:, part], mask=inside[:, part])


def shifted(buf, k, base, sign):
    dr, dc = sign * ROW_STEP[k], sign * COL_STEP[k]
    x = [buf[k, l, pl.ds(base + dr, 8), :] for l in range(LANES)]
    if dc == 1:
        x = x[1:] + [pltpu.roll(x[0], 127, 1)]
    if dc == -1:
        x = [pltpu.roll(x[-1], 1, 1)] + x[:-1]
    return jnp.concatenate(x, axis=1)


def mix(mat, tiles):
    x = jnp.concatenate([jnp.concatenate([p[k] for p in tiles], axis=1) for k in range(8)], axis=0)
    hi = x.astype(jnp.bfloat16)
    lo = (x - hi.astype(jnp.float32)).astype(jnp.bfloat16)
    y = jnp.dot(mat, jnp.concatenate([hi, lo], axis=0), preferred_element_type=jnp.float32)
    return [[y[8 * k : 8 * k + 8, WIDE * u : WIDE * (u + 1)] for k in range(8)] for u in range(len(tiles))]


def reach(radius):
    return (radius + 7) // 8


def span(radius):
    far = (radius + 7) // 8
    return REACH - far + 1, REACH + far + 2


def main_kernel(
    pos_ref, moves_ref, back_ref, forth_ref, hot_ref, up_ref, mid_ref, down_ref, cost_ref, values_ref, visits_ref,
    damp, start, even, odd, held, lowest, total_visits, final, stack, picked, gathered,
):
    pos = pos_ref[0]
    lane = column_of(lax.broadcasted_iota(jnp.int32, (8, WIDE), 1))
    sub = lax.broadcasted_iota(jnp.int32, (8, WIDE), 0)
    zero = jnp.zeros((8, WIDE), jnp.float32)
    one = jnp.full((8, WIDE), Z_SCALE, jnp.float32)
    for k in range(8):
        for edge in (0, TILES + 1):
            put(even, k, 8 * edge, one)
            put(odd, k, 8 * edge, one)

    def fetch(src, at, tile, raw):
        block = src[at]
        enter, pen, mass = block[0:8], block[8:16], block[16:24]
        base = pl.multiple_of(8 * tile, 8)
        inside = enter > 0.0
        row = 8 * tile + sub - 8 * (REACH + 1)
        near = (row >= -20) & (row < TR + 20) & (lane >= EDGE - 20) & (lane < EDGE + TC + 20)
        start[pl.ds(base, 8), :] = jnp.where(near, mass, 0.0)
        if raw:
            damp[pl.ds(base, 8), :] = enter
            first = pen
        else:
            damp[pl.ds(base, 8), :] = jnp.where(inside, jnp.exp(-enter), 0.0)
            first = jnp.exp(pen) * Z_SCALE
        for k in range(8):
            put(even, k, base, first)
            put(odd, k, base, first)

    def load_window(raw):
        def body(tile, carry):
            at = pos + tile - 1

            @pl.when(at < REACH)
            def _():
                fetch(up_ref, at, tile, raw)

            @pl.when((at >= REACH) & (at < REACH + GROUP))
            def _():
                fetch(mid_ref, at - REACH, tile, raw)

            @pl.when(at >= REACH + GROUP)
            def _():
                fetch(down_ref, at - REACH - GROUP, tile, raw)

            return carry

        lax.fori_loop(1, TILES + 1, body, 0)

    load_window(False)

    back, forth = back_ref[...], forth_ref[...]
    mine = 8 * (REACH + 1)

    center = REACH + 1

    def over_tiles(far, work):
        tiles = list(range(center - far, center + far + 1))
        for first in range(0, len(tiles), CHUNK):
            work([8 * tile for tile in tiles[first : first + CHUNK]])

    def in_pairs(first, last, sources, far, step):
        def turn(n, carry):
            step(first + 2 * n, sources[0], sources[1], far)
            step(first + 2 * n + 1, sources[1], sources[0], far)
            return carry

        lax.fori_loop(0, (last - first) // 2, turn, 0)

    def back_step(n, now, later, far):
        t = ITERS - 1 - n

        def work(bases):
            totals = mix(back, [[shifted(now, k, b, 1) for k in range(8)] for b in bases])
            for b, total in zip(bases, totals):
                e = damp[pl.ds(b, 8), :]
                inside = e > 0.0
                for k in range(8):
                    z = total[k] * e
                    put_inside(later, k, b, z, inside)
                    if b == mine:
                        held[t, k] = z

        over_tiles(far, work)

    for k in range(8):
        held[ITERS, k] = take(even, k, mine)
    in_pairs(0, 8, (even, odd), 5, back_step)
    in_pairs(8, 16, (even, odd), 4, back_step)
    in_pairs(16, 18, (even, odd), 3, back_step)
    back_step(18, even, odd, 3)
    lowest[...] = one

    def turn(bases):
        totals = mix(back, [[shifted(odd, k, b, 1) for k in range(8)] for b in bases])
        share = []
        for b, total in zip(bases, totals):
            row = b + sub - mine
            near = (row >= -20) & (row < TR + 20) & (lane >= EDGE - 20) & (lane < EDGE + TC + 20)
            live = near & (damp[pl.ds(b, 8), :] > 0.0)
            low = total[0]
            for k in range(1, 8):
                low = jnp.minimum(low, total[k])
            lowest[...] = jnp.minimum(lowest[...], jnp.where(live, low, Z_SCALE))
            mass = start[pl.ds(b, 8), :] * Y_SCALE
            live = live & (mass > 0.0)
            share.append([jnp.where(live, mass / z, 0.0) for z in total])
            if b == mine:
                for k in range(8):
                    final[8 * k : 8 * k + 8, :] = jnp.log(total[k] * (1.0 / Z_SCALE))
        flows = mix(forth, share)
        for b, flow in zip(bases, flows):
            for k in range(8):
                put(even, k, b, flow[k])

    over_tiles(3, turn)
    for k in range(8):
        for tile in (center - 4, center + 4):
            put(even, k, 8 * tile, zero)
            put(odd, k, 8 * tile, zero)
    good = jnp.min(lowest[...]) >= Z_FLOOR

    total_visits[...] = zero

    def forth_step(t, now, later, far):
        def work(bases):
            arrive = [[shifted(now, k, b, -1) for k in range(8)] for b in bases]
            if mine in bases:
                total = total_visits[...]
                for k in range(8):
                    total = total + arrive[bases.index(mine)][k] * held[t + 1, k]
                total_visits[...] = total
            damps = [damp[pl.ds(b, 8), :] for b in bases]
            flows = mix(forth, [[x * e for x in part] for e, part in zip(damps, arrive)])
            for b, flow in zip(bases, flows):
                for k in range(8):
                    put(later, k, b, flow[k])

        over_tiles(far, work)

    in_pairs(0, 4, (even, odd), 3, forth_step)
    in_pairs(4, 12, (even, odd), 2, forth_step)
    in_pairs(12, 18, (even, odd), 1, forth_step)
    forth_step(18, even, odd, 1)
    total = total_visits[...]
    for k in range(8):
        total = total + shifted(odd, k, mine, -1) * held[ITERS, k]
    final[64:72, :] = total * (1.0 / Y_SCALE)

    @pl.when(jnp.logical_not(good))
    def _():
        load_window(True)

        def log_total(h):
            most = picked[moves_ref[h, 0]]
            for a in range(1, 8):
                most = jnp.maximum(most, picked[moves_ref[h, a]])
            part = zero
            for a in range(8):
                part = part + jnp.exp(picked[moves_ref[h, a]] - most)
            return most + jnp.log(part)

        for tile in (0, TILES + 1):
            for k in range(8):
                put(even, k, 8 * tile, zero)

        def settle():
            def body(tile, carry):
                base = pl.multiple_of(8 * tile, 8)
                for k in range(8):
                    put(even, k, base, take(odd, k, base))
                return carry

            lax.fori_loop(1, TILES + 1, body, 0)

        def slow_back(n, carry):
            t = ITERS - 1 - n

            def keep(tile, carry):
                base = pl.multiple_of(8 * tile, 8)
                for k in range(8):
                    put(stack.at[n], k, pl.multiple_of(base - 16, 8), take(even, k, base))
                return carry

            lax.fori_loop(2, TILES, keep, 0)
            far = reach(t + 20)
            lo, hi = center - far, center + far + 1

            def tile_step(tile, carry):
                base = pl.multiple_of(8 * tile, 8)
                for k in range(8):
                    picked[k] = shifted(even, k, base, 1)
                enter = damp[pl.ds(base, 8), :]

                def heading(h, carry):
                    total = log_total(h)
                    put(odd, h, base, jnp.where(enter > 0.0, total - enter, 0.0))

                    @pl.when((t == 0) & (tile == REACH + 1))
                    def _():
                        final[pl.ds(pl.multiple_of(8 * h, 8), 8), :] = total

                    return carry

                return lax.fori_loop(0, 8, heading, carry)

            lax.fori_loop(lo, hi, tile_step, 0)
            settle()
            return carry

        lax.fori_loop(0, ITERS, slow_back, 0)
        for k in range(8):
            for tile in range(TILES + 2):
                put(even, k, 8 * tile, zero)
                put(odd, k, 8 * tile, zero)

        def slow_forth(t, visits):
            far = reach(ITERS - t)
            lo, hi = center - far, center + far + 1

            def tile_step(tile, carry):
                base = pl.multiple_of(8 * tile, 8)
                inside = damp[pl.ds(base, 8), :] > 0.0
                mass = start[pl.ds(base, 8), :]
                for k in range(8):
                    picked[k] = shifted(stack.at[ITERS - 1 - t], k, pl.multiple_of(base - 16, 8), 1)
                    gathered[k] = zero
                    come = jnp.where(inside, shifted(even, k, base, -1), 0.0)
                    gathered[8 + k] = jnp.where(t == 0, mass, come)

                def heading(h, carry):
                    total = log_total(h)
                    here = gathered[8 + h]
                    for a in range(8):
                        k = moves_ref[h, a]
                        gathered[k] = gathered[k] + here * jnp.exp(picked[k] - total)
                    return carry

                lax.fori_loop(0, 8, heading, 0)
                for k in range(8):
                    put(odd, k, base, gathered[k])
                return carry

            lax.fori_loop(lo, hi, tile_step, 0)
            settle()
            total = zero
            for k in range(8):
                total = total + shifted(even, k, mine, -1)
            return visits + total

        visits = lax.fori_loop(0, ITERS, slow_forth, zero)
        final[64:72, :] = visits

    out = moved(final[...], hot_ref[...])
    for k in range(8):
        values_ref[k] = (out[8 * k : 8 * k + 8] - cost_ref[...]) / ITERS
    visits_ref[...] = out[64:72]


def window_call(pos, move_table, back, forth, hot, up, mid, down, cell_cost):
    smem = pl.BlockSpec(memory_space=pltpu.SMEM)
    vmem = pl.BlockSpec(memory_space=pltpu.VMEM)
    rows = 8 * (TILES + 2)
    return pl.pallas_call(
        main_kernel,
        in_specs=[smem, smem] + [vmem] * 7,
        out_specs=[vmem, vmem],
        out_shape=[
            jax.ShapeDtypeStruct((8, TR, TC), jnp.float32),
            jax.ShapeDtypeStruct((TR, TC), jnp.float32),
        ],
        scratch_shapes=[
            pltpu.VMEM((rows, WIDE), jnp.float32),
            pltpu.VMEM((rows, WIDE), jnp.float32),
            pltpu.VMEM((8, LANES, rows, 128), jnp.float32),
            pltpu.VMEM((8, LANES, rows, 128), jnp.float32),
            pltpu.VMEM((ITERS + 1, 8, 8, WIDE), jnp.float32),
            pltpu.VMEM((8, WIDE), jnp.float32),
            pltpu.VMEM((8, WIDE), jnp.float32),
            pltpu.VMEM((72, WIDE), jnp.float32),
            pltpu.VMEM((ITERS, 8, LANES, 72, 128), jnp.float32),
            pltpu.VMEM((8, 8, WIDE), jnp.float32),
            pltpu.VMEM((16, 8, WIDE), jnp.float32),
        ],
        compiler_params=pltpu.CompilerParams(vmem_limit_bytes=50 * 2**20),
        name="raster_steps",
    )(pos, move_table, back, forth, hot, up, mid, down, cell_cost)


def prepare_call(cell_cost, blocked, cells, mass):
    edge = jax.ShapeDtypeStruct((24, EDGE), jnp.float32)
    return pl.pallas_call(
        prepare_kernel,
        out_shape=[jax.ShapeDtypeStruct((24, TC), jnp.float32), edge, edge],
        name="raster_prepare",
    )(cell_cost, blocked, cells, mass)


def aside_call(own, move_table):
    matrix = jax.ShapeDtypeStruct((64, 128), jnp.bfloat16)
    return pl.pallas_call(
        aside_kernel,
        out_shape=[
            jax.ShapeDtypeStruct((24, WIDE), jnp.float32), matrix, matrix,
            jax.ShapeDtypeStruct((WIDE, TC), jnp.bfloat16),
        ],
        cost_estimate=pl.CostEstimate(flops=2 * 72 * TC * WIDE, bytes_accessed=2**20, transcendentals=0),
        name="raster_aside",
    )(own, move_table)


def strip_call(left, right, own):
    return pl.pallas_call(
        strip_kernel,
        out_shape=jax.ShapeDtypeStruct((24, WIDE), jnp.float32),
        name="raster_strip",
    )(left, right, own)


def on_device(cell_cost, blocked, move_table, anchor_cells, anchor_mass):
    n_rows, n_cols = lax.axis_size("rows"), lax.axis_size("cols")
    own, first, last = prepare_call(
        cell_cost, blocked, anchor_cells.reshape(1, 128), anchor_mass.reshape(1, 128)
    )
    left = lax.ppermute(last, "cols", [(i, i + 1) for i in range(n_cols - 1)])
    right = lax.ppermute(first, "cols", [(i + 1, i) for i in range(n_cols - 1)])
    own, back, forth, hot = aside_call(own, move_table)
    strip = strip_call(left, right, own)
    groups = [list(range(g, g + GROUP)) for g in range(0, n_rows, GROUP)]
    mid = lax.all_gather(strip, "rows", axis_index_groups=groups)
    up = lax.ppermute(mid[GROUP - REACH :], "rows", [(i, i + GROUP) for i in range(n_rows - GROUP)])
    down = lax.ppermute(mid[:REACH], "rows", [(i + GROUP, i) for i in range(n_rows - GROUP)])
    pos = lax.rem(lax.axis_index("rows"), GROUP).astype(jnp.int32).reshape(1)
    values, visits = window_call(pos, move_table, back, forth, hot, up, mid, down, cell_cost)
    return values, visits


def solution(mesh):
    placed = (
        P("rows", "cols"),
        P("rows", "cols"),
        P(),
        P("rows", "cols", None),
        P("rows", "cols", None),
    )
    return jax.shard_map(
        on_device,
        mesh=mesh,
        in_specs=placed,
        out_specs=(P(None, "rows", "cols"), P("rows", "cols")),
        check_vma=False,
    )
```

```python
import functools

import jax
import jax.numpy as jnp
from jax import lax
from jax.experimental import pallas as pl
from jax.experimental.pallas import tpu as pltpu
from jax.sharding import PartitionSpec as P

ITERS = 20
PENALTY = 3.0
ROW_STEP = (0, -1, -1, -1, 0, 1, 1, 1)
COL_STEP = (1, 1, 0, -1, -1, -1, 0, 1)
TR, TC = 8, 512
REACH = 5
EDGE = 64
WIDE = TC + 2 * EDGE
LANES = WIDE // 128
TILES = 2 * REACH + 1
BARE = 2
GROUP = 8
CHUNK = 2
Z_SCALE = 2.0**60
Y_SCALE = 2.0**30
Z_FLOOR = 2.0**-36


def terms(x):
    first = x.astype(jnp.bfloat16)
    rest = x - first.astype(jnp.float32)
    second = rest.astype(jnp.bfloat16)
    third = (rest - second.astype(jnp.float32)).astype(jnp.bfloat16)
    return jnp.concatenate([first, second, third], axis=0)


def summed(y, n):
    return y[:n] + (y[n : 2 * n] + y[2 * n :])


def prepare_kernel(cost_ref, blocked_ref, cells_ref, mass_ref, own_ref, first_ref, last_ref):
    penalty = -PENALTY * blocked_ref[...].astype(jnp.float32)
    cells = cells_ref[...]
    row = lax.broadcasted_iota(jnp.int32, (TR, 128), 0)
    weight = jnp.where(row == (cells >> 9), mass_ref[...] * 0.125, 0.0)
    col = lax.broadcasted_iota(jnp.int32, (TC, 128), 0)
    hot = jnp.where(col == (cells & (TC - 1)), 1.0, 0.0).astype(jnp.bfloat16)
    start = summed(
        lax.dot_general(terms(weight), hot, (((1,), (1,)), ((), ())), preferred_element_type=jnp.float32), TR
    )
    own = jnp.concatenate([cost_ref[...] - penalty, penalty, start], axis=0)
    own_ref[...] = own
    first_ref[...] = own[:, :EDGE]
    last_ref[...] = own[:, TC - EDGE :]


def column_of(place):
    return LANES * (place & 127) + (place >> 7)


def moved(x, hot):
    return summed(jnp.dot(terms(x), hot, preferred_element_type=jnp.float32), x.shape[0])


def hot_matrix(columns, wide):
    place = lax.broadcasted_iota(jnp.int32, (columns.shape[0], wide), 1)
    return jnp.where(columns == column_of(place), 1.0, 0.0).astype(jnp.bfloat16)


def aside_kernel(own_ref, table_ref, out_ref, back_ref, forth_ref, hot_ref):
    column = lax.broadcasted_iota(jnp.int32, (TC, WIDE), 0) + EDGE
    out_ref[...] = moved(own_ref[...], hot_matrix(column, WIDE))
    table = jnp.broadcast_to(table_ref[...].reshape(8, 1, 8), (8, 8, 8)).reshape(64, 8)
    col = lax.broadcasted_iota(jnp.int32, (64, 64), 1)
    row = lax.broadcasted_iota(jnp.int32, (64, 64), 0)
    count = jnp.zeros((64, 64), jnp.float32)
    for a in range(8):
        count = count + jnp.where(table[:, a : a + 1] == (col >> 3), 1.0, 0.0)
    count = jnp.where((row & 7) == (col & 7), count, 0.0)
    turned = count.T
    back_ref[...] = jnp.concatenate([count, count], axis=1).astype(jnp.bfloat16)
    forth_ref[...] = jnp.concatenate([turned, turned], axis=1).astype(jnp.bfloat16)
    place = lax.broadcasted_iota(jnp.int32, (WIDE, TC), 0)
    column = lax.broadcasted_iota(jnp.int32, (WIDE, TC), 1) + EDGE
    hot_ref[...] = jnp.where(column_of(place) == column, 1.0, 0.0).astype(jnp.bfloat16)


def strip_kernel(left_ref, right_ref, own_ref, out_ref):
    x = jnp.concatenate([left_ref[...], right_ref[...]], axis=1)
    column = lax.broadcasted_iota(jnp.int32, (2 * EDGE, WIDE), 0)
    column = jnp.where(column < EDGE, column, column + TC)
    out_ref[...] = own_ref[...] + moved(x, hot_matrix(column, WIDE))


def take(buf, k, base):
    return jnp.concatenate([buf[k, l, pl.ds(base, 8), :] for l in range(LANES)], axis=1)


def put(buf, k, base, x):
    for l in range(LANES):
        buf[k, l, pl.ds(base, 8), :] = x[:, 128 * l : 128 * l + 128]


def put_inside(buf, k, base, x, inside):
    for l in range(LANES):
        part = slice(128 * l, 128 * l + 128)
        pltpu.store(buf.at[k, l, pl.ds(base, 8), :], x[:, part], mask=inside[:, part])


def shifted(buf, k, base, sign):
    dr, dc = sign * ROW_STEP[k], sign * COL_STEP[k]
    x = [buf[k, l, pl.ds(base + dr, 8), :] for l in range(LANES)]
    if dc == 1:
        x = x[1:] + [pltpu.roll(x[0], 127, 1)]
    if dc == -1:
        x = [pltpu.roll(x[-1], 1, 1)] + x[:-1]
    return jnp.concatenate(x, axis=1)


def mix(mat, tiles):
    x = jnp.concatenate([jnp.concatenate([p[k] for p in tiles], axis=1) for k in range(8)], axis=0)
    hi = x.astype(jnp.bfloat16)
    lo = (x - hi.astype(jnp.float32)).astype(jnp.bfloat16)
    y = jnp.dot(mat, jnp.concatenate([hi, lo], axis=0), preferred_element_type=jnp.float32)
    return [[y[8 * k : 8 * k + 8, WIDE * u : WIDE * (u + 1)] for k in range(8)] for u in range(len(tiles))]


def reach(radius):
    return (radius + 7) // 8


def span(radius):
    far = (radius + 7) // 8
    return REACH - far + 1, REACH + far + 2


def main_kernel(
    pos_ref, moves_ref, back_ref, forth_ref, hot_ref, up_ref, mid_ref, down_ref, cost_ref, values_ref, visits_ref,
    damp, start, even, odd, held, lowest, total_visits, final, stack, picked, gathered,
):
    pos = pos_ref[0]
    lane = column_of(lax.broadcasted_iota(jnp.int32, (8, WIDE), 1))
    sub = lax.broadcasted_iota(jnp.int32, (8, WIDE), 0)
    zero = jnp.zeros((8, WIDE), jnp.float32)
    one = jnp.full((8, WIDE), Z_SCALE, jnp.float32)
    for k in range(8):
        for edge in (0, TILES + 1):
            put(even, k, 8 * edge, one)
            put(odd, k, 8 * edge, one)

    def fetch(block, tile, raw):
        enter, pen = block[0:8], block[8:16]
        mass = block[16:24] if block.shape[0] == 24 else zero
        base = pl.multiple_of(8 * tile, 8)
        inside = enter > 0.0
        row = 8 * tile + sub - 8 * (REACH + 1)
        near = (row >= -20) & (row < TR + 20) & (lane >= EDGE - 20) & (lane < EDGE + TC + 20)
        start[pl.ds(base, 8), :] = jnp.where(near, mass, 0.0)
        if raw:
            damp[pl.ds(base, 8), :] = enter
            first = pen
        else:
            damp[pl.ds(base, 8), :] = jnp.where(inside, jnp.exp(-enter), 0.0)
            first = jnp.exp(pen) * Z_SCALE
        for k in range(8):
            put(even, k, base, first)
            put(odd, k, base, first)

    def load_window(raw):
        def body(tile, carry):
            at = pos + tile - 1

            below = at - REACH - GROUP

            @pl.when(at < BARE)
            def _():
                fetch(up_ref[pl.ds(pl.multiple_of(16 * at, 8), 16), :], tile, raw)

            @pl.when((at >= BARE) & (at < REACH))
            def _():
                row = pl.multiple_of(16 * BARE + 24 * (at - BARE), 8)
                fetch(up_ref[pl.ds(row, 24), :], tile, raw)

            @pl.when((at >= REACH) & (below < 0))
            def _():
                fetch(mid_ref[at - REACH], tile, raw)

            @pl.when((below >= 0) & (below < REACH - BARE))
            def _():
                fetch(down_ref[pl.ds(pl.multiple_of(24 * below, 8), 24), :], tile, raw)

            @pl.when(below >= REACH - BARE)
            def _():
                row = pl.multiple_of(24 * (REACH - BARE) + 16 * (below - REACH + BARE), 8)
                fetch(down_ref[pl.ds(row, 16), :], tile, raw)

            return carry

        lax.fori_loop(1, TILES + 1, body, 0)

    load_window(False)

    back, forth = back_ref[...], forth_ref[...]
    mine = 8 * (REACH + 1)

    center = REACH + 1

    def over_tiles(far, work):
        tiles = list(range(center - far, center + far + 1))
        for first in range(0, len(tiles), CHUNK):
            work([8 * tile for tile in tiles[first : first + CHUNK]])

    def in_pairs(first, last, sources, far, step):
        def turn(n, carry):
            step(first + 2 * n, sources[0], sources[1], far)
            step(first + 2 * n + 1, sources[1], sources[0], far)
            return carry

        lax.fori_loop(0, (last - first) // 2, turn, 0)

    def back_step(n, now, later, far):
        t = ITERS - 1 - n

        def work(bases):
            totals = mix(back, [[shifted(now, k, b, 1) for k in range(8)] for b in bases])
            for b, total in zip(bases, totals):
                e = damp[pl.ds(b, 8), :]
                inside = e > 0.0
                for k in range(8):
                    z = total[k] * e
                    put_inside(later, k, b, z, inside)
                    if b == mine:
                        held[t, k] = z

        over_tiles(far, work)

    for k in range(8):
        held[ITERS, k] = take(even, k, mine)
    in_pairs(0, 8, (even, odd), 5, back_step)
    in_pairs(8, 16, (even, odd), 4, back_step)
    in_pairs(16, 18, (even, odd), 3, back_step)
    back_step(18, even, odd, 3)
    lowest[...] = one

    def turn(bases):
        totals = mix(back, [[shifted(odd, k, b, 1) for k in range(8)] for b in bases])
        share = []
        for b, total in zip(bases, totals):
            row = b + sub - mine
            near = (row >= -20) & (row < TR + 20) & (lane >= EDGE - 20) & (lane < EDGE + TC + 20)
            live = near & (damp[pl.ds(b, 8), :] > 0.0)
            low = total[0]
            for k in range(1, 8):
                low = jnp.minimum(low, total[k])
            lowest[...] = jnp.minimum(lowest[...], jnp.where(live, low, Z_SCALE))
            mass = start[pl.ds(b, 8), :] * Y_SCALE
            live = live & (mass > 0.0)
            share.append([jnp.where(live, mass / z, 0.0) for z in total])
            if b == mine:
                for k in range(8):
                    final[8 * k : 8 * k + 8, :] = jnp.log(total[k] * (1.0 / Z_SCALE))
        flows = mix(forth, share)
        for b, flow in zip(bases, flows):
            for k in range(8):
                put(even, k, b, flow[k])

    over_tiles(3, turn)
    for k in range(8):
        for tile in (center - 4, center + 4):
            put(even, k, 8 * tile, zero)
            put(odd, k, 8 * tile, zero)
    good = jnp.min(lowest[...]) >= Z_FLOOR

    total_visits[...] = zero

    def forth_step(t, now, later, far):
        def work(bases):
            arrive = [[shifted(now, k, b, -1) for k in range(8)] for b in bases]
            if mine in bases:
                total = total_visits[...]
                for k in range(8):
                    total = total + arrive[bases.index(mine)][k] * held[t + 1, k]
                total_visits[...] = total
            damps = [damp[pl.ds(b, 8), :] for b in bases]
            flows = mix(forth, [[x * e for x in part] for e, part in zip(damps, arrive)])
            for b, flow in zip(bases, flows):
                for k in range(8):
                    put(later, k, b, flow[k])

        over_tiles(far, work)

    in_pairs(0, 4, (even, odd), 3, forth_step)
    in_pairs(4, 12, (even, odd), 2, forth_step)
    in_pairs(12, 18, (even, odd), 1, forth_step)
    forth_step(18, even, odd, 1)
    total = total_visits[...]
    for k in range(8):
        total = total + shifted(odd, k, mine, -1) * held[ITERS, k]
    final[64:72, :] = total * (1.0 / Y_SCALE)

    @pl.when(jnp.logical_not(good))
    def _():
        load_window(True)

        def log_total(h):
            most = picked[moves_ref[h, 0]]
            for a in range(1, 8):
                most = jnp.maximum(most, picked[moves_ref[h, a]])
            part = zero
            for a in range(8):
                part = part + jnp.exp(picked[moves_ref[h, a]] - most)
            return most + jnp.log(part)

        for tile in (0, TILES + 1):
            for k in range(8):
                put(even, k, 8 * tile, zero)

        def settle():
            def body(tile, carry):
                base = pl.multiple_of(8 * tile, 8)
                for k in range(8):
                    put(even, k, base, take(odd, k, base))
                return carry

            lax.fori_loop(1, TILES + 1, body, 0)

        def slow_back(n, carry):
            t = ITERS - 1 - n

            def keep(tile, carry):
                base = pl.multiple_of(8 * tile, 8)
                for k in range(8):
                    put(stack.at[n], k, pl.multiple_of(base - 16, 8), take(even, k, base))
                return carry

            lax.fori_loop(2, TILES, keep, 0)
            far = reach(t + 20)
            lo, hi = center - far, center + far + 1

            def tile_step(tile, carry):
                base = pl.multiple_of(8 * tile, 8)
                for k in range(8):
                    picked[k] = shifted(even, k, base, 1)
                enter = damp[pl.ds(base, 8), :]

                def heading(h, carry):
                    total = log_total(h)
                    put(odd, h, base, jnp.where(enter > 0.0, total - enter, 0.0))

                    @pl.when((t == 0) & (tile == REACH + 1))
                    def _():
                        final[pl.ds(pl.multiple_of(8 * h, 8), 8), :] = total

                    return carry

                return lax.fori_loop(0, 8, heading, carry)

            lax.fori_loop(lo, hi, tile_step, 0)
            settle()
            return carry

        lax.fori_loop(0, ITERS, slow_back, 0)
        for k in range(8):
            for tile in range(TILES + 2):
                put(even, k, 8 * tile, zero)
                put(odd, k, 8 * tile, zero)

        def slow_forth(t, visits):
            far = reach(ITERS - t)
            lo, hi = center - far, center + far + 1

            def tile_step(tile, carry):
                base = pl.multiple_of(8 * tile, 8)
                inside = damp[pl.ds(base, 8), :] > 0.0
                mass = start[pl.ds(base, 8), :]
                for k in range(8):
                    picked[k] = shifted(stack.at[ITERS - 1 - t], k, pl.multiple_of(base - 16, 8), 1)
                    gathered[k] = zero
                    come = jnp.where(inside, shifted(even, k, base, -1), 0.0)
                    gathered[8 + k] = jnp.where(t == 0, mass, come)

                def heading(h, carry):
                    total = log_total(h)
                    here = gathered[8 + h]
                    for a in range(8):
                        k = moves_ref[h, a]
                        gathered[k] = gathered[k] + here * jnp.exp(picked[k] - total)
                    return carry

                lax.fori_loop(0, 8, heading, 0)
                for k in range(8):
                    put(odd, k, base, gathered[k])
                return carry

            lax.fori_loop(lo, hi, tile_step, 0)
            settle()
            total = zero
            for k in range(8):
                total = total + shifted(even, k, mine, -1)
            return visits + total

        visits = lax.fori_loop(0, ITERS, slow_forth, zero)
        final[64:72, :] = visits

    out = moved(final[...], hot_ref[...])
    for k in range(8):
        values_ref[k] = (out[8 * k : 8 * k + 8] - cost_ref[...]) / ITERS
    visits_ref[...] = out[64:72]


def window_call(pos, move_table, back, forth, hot, up, mid, down, cell_cost):
    smem = pl.BlockSpec(memory_space=pltpu.SMEM)
    vmem = pl.BlockSpec(memory_space=pltpu.VMEM)
    rows = 8 * (TILES + 2)
    return pl.pallas_call(
        main_kernel,
        in_specs=[smem, smem] + [vmem] * 7,
        out_specs=[vmem, vmem],
        out_shape=[
            jax.ShapeDtypeStruct((8, TR, TC), jnp.float32),
            jax.ShapeDtypeStruct((TR, TC), jnp.float32),
        ],
        scratch_shapes=[
            pltpu.VMEM((rows, WIDE), jnp.float32),
            pltpu.VMEM((rows, WIDE), jnp.float32),
            pltpu.VMEM((8, LANES, rows, 128), jnp.float32),
            pltpu.VMEM((8, LANES, rows, 128), jnp.float32),
            pltpu.VMEM((ITERS + 1, 8, 8, WIDE), jnp.float32),
            pltpu.VMEM((8, WIDE), jnp.float32),
            pltpu.VMEM((8, WIDE), jnp.float32),
            pltpu.VMEM((72, WIDE), jnp.float32),
            pltpu.VMEM((ITERS, 8, LANES, 72, 128), jnp.float32),
            pltpu.VMEM((8, 8, WIDE), jnp.float32),
            pltpu.VMEM((16, 8, WIDE), jnp.float32),
        ],
        compiler_params=pltpu.CompilerParams(vmem_limit_bytes=50 * 2**20),
        name="raster_steps",
    )(pos, move_table, back, forth, hot, up, mid, down, cell_cost)


def prepare_call(cell_cost, blocked, cells, mass):
    edge = jax.ShapeDtypeStruct((24, EDGE), jnp.float32)
    return pl.pallas_call(
        prepare_kernel,
        out_shape=[jax.ShapeDtypeStruct((24, TC), jnp.float32), edge, edge],
        name="raster_prepare",
    )(cell_cost, blocked, cells, mass)


def aside_call(own, move_table):
    matrix = jax.ShapeDtypeStruct((64, 128), jnp.bfloat16)
    return pl.pallas_call(
        aside_kernel,
        out_shape=[
            jax.ShapeDtypeStruct((24, WIDE), jnp.float32), matrix, matrix,
            jax.ShapeDtypeStruct((WIDE, TC), jnp.bfloat16),
        ],
        cost_estimate=pl.CostEstimate(flops=2 * 72 * TC * WIDE, bytes_accessed=2**20, transcendentals=0),
        name="raster_aside",
    )(own, move_table)


def strip_call(left, right, own):
    return pl.pallas_call(
        strip_kernel,
        out_shape=jax.ShapeDtypeStruct((24, WIDE), jnp.float32),
        name="raster_strip",
    )(left, right, own)


def halos(mid):
    near = REACH - BARE
    above = [mid[GROUP - REACH : GROUP - near, :16].reshape(16 * BARE, WIDE), mid[GROUP - near :].reshape(24 * near, WIDE)]
    below = [mid[:near].reshape(24 * near, WIDE), mid[near:REACH, :16].reshape(16 * BARE, WIDE)]
    return jnp.concatenate(above, axis=0), jnp.concatenate(below, axis=0)


def on_device(cell_cost, blocked, move_table, anchor_cells, anchor_mass):
    n_rows, n_cols = lax.axis_size("rows"), lax.axis_size("cols")
    own, first, last = prepare_call(
        cell_cost, blocked, anchor_cells.reshape(1, 128), anchor_mass.reshape(1, 128)
    )
    left = lax.ppermute(last, "cols", [(i, i + 1) for i in range(n_cols - 1)])
    right = lax.ppermute(first, "cols", [(i + 1, i) for i in range(n_cols - 1)])
    own, back, forth, hot = aside_call(own, move_table)
    strip = strip_call(left, right, own)
    groups = [list(range(g, g + GROUP)) for g in range(0, n_rows, GROUP)]
    mid = lax.all_gather(strip, "rows", axis_index_groups=groups)
    above, below = halos(mid)
    up = lax.ppermute(above, "rows", [(i, i + GROUP) for i in range(n_rows - GROUP)])
    down = lax.ppermute(below, "rows", [(i + GROUP, i) for i in range(n_rows - GROUP)])
    pos = lax.rem(lax.axis_index("rows"), GROUP).astype(jnp.int32).reshape(1)
    values, visits = window_call(pos, move_table, back, forth, hot, up, mid, down, cell_cost)
    return values, visits


def solution(mesh):
    placed = (
        P("rows", "cols"),
        P("rows", "cols"),
        P(),
        P("rows", "cols", None),
        P("rows", "cols", None),
    )
    return jax.shard_map(
        on_device,
        mesh=mesh,
        in_specs=placed,
        out_specs=(P(None, "rows", "cols"), P("rows", "cols")),
        check_vma=False,
    )
```

```python
import functools

import jax
import jax.numpy as jnp
from jax import lax
from jax.experimental import pallas as pl
from jax.experimental.pallas import tpu as pltpu
from jax.sharding import PartitionSpec as P

ITERS = 20
PENALTY = 3.0
ROW_STEP = (0, -1, -1, -1, 0, 1, 1, 1)
COL_STEP = (1, 1, 0, -1, -1, -1, 0, 1)
TR, TC = 8, 512
REACH = 5
EDGE = 64
WIDE = TC + 2 * EDGE
LANES = WIDE // 128
TILES = 2 * REACH + 1
BARE = 2
GROUP = 8
CHUNK = 2
Z_SCALE = 2.0**60
Y_SCALE = 2.0**30
Z_FLOOR = 2.0**-36


def terms(x):
    first = x.astype(jnp.bfloat16)
    rest = x - first.astype(jnp.float32)
    second = rest.astype(jnp.bfloat16)
    third = (rest - second.astype(jnp.float32)).astype(jnp.bfloat16)
    return jnp.concatenate([first, second, third], axis=0)


def summed(y, n):
    return y[:n] + (y[n : 2 * n] + y[2 * n :])


def prepare_kernel(cost_ref, blocked_ref, cells_ref, mass_ref, own_ref, first_ref, last_ref):
    penalty = -PENALTY * blocked_ref[...].astype(jnp.float32)
    cells = cells_ref[...]
    row = lax.broadcasted_iota(jnp.int32, (TR, 128), 0)
    weight = jnp.where(row == (cells >> 9), mass_ref[...] * 0.125, 0.0)
    col = lax.broadcasted_iota(jnp.int32, (TC, 128), 0)
    hot = jnp.where(col == (cells & (TC - 1)), 1.0, 0.0).astype(jnp.bfloat16)
    start = summed(
        lax.dot_general(terms(weight), hot, (((1,), (1,)), ((), ())), preferred_element_type=jnp.float32), TR
    )
    own = jnp.concatenate([cost_ref[...] - penalty, penalty, start], axis=0)
    own_ref[...] = own
    column = lax.broadcasted_iota(jnp.int32, (EDGE, WIDE), 0)
    first_ref[...] = moved(own[:, :EDGE], hot_matrix(column + EDGE + TC, WIDE))
    last_ref[...] = moved(own[:, TC - EDGE :], hot_matrix(column, WIDE))


def column_of(place):
    return LANES * (place & 127) + (place >> 7)


def moved(x, hot):
    return summed(jnp.dot(terms(x), hot, preferred_element_type=jnp.float32), x.shape[0])


def hot_matrix(columns, wide):
    place = lax.broadcasted_iota(jnp.int32, (columns.shape[0], wide), 1)
    return jnp.where(columns == column_of(place), 1.0, 0.0).astype(jnp.bfloat16)


def aside_kernel(own_ref, table_ref, out_ref, back_ref, forth_ref, hot_ref):
    column = lax.broadcasted_iota(jnp.int32, (TC, WIDE), 0) + EDGE
    out_ref[...] = moved(own_ref[...], hot_matrix(column, WIDE))
    table = jnp.broadcast_to(table_ref[...].reshape(8, 1, 8), (8, 8, 8)).reshape(64, 8)
    col = lax.broadcasted_iota(jnp.int32, (64, 64), 1)
    row = lax.broadcasted_iota(jnp.int32, (64, 64), 0)
    count = jnp.zeros((64, 64), jnp.float32)
    for a in range(8):
        count = count + jnp.where(table[:, a : a + 1] == (col >> 3), 1.0, 0.0)
    count = jnp.where((row & 7) == (col & 7), count, 0.0)
    turned = count.T
    back_ref[...] = jnp.concatenate([count, count], axis=1).astype(jnp.bfloat16)
    forth_ref[...] = jnp.concatenate([turned, turned], axis=1).astype(jnp.bfloat16)
    place = lax.broadcasted_iota(jnp.int32, (WIDE, TC), 0)
    column = lax.broadcasted_iota(jnp.int32, (WIDE, TC), 1) + EDGE
    hot_ref[...] = jnp.where(column_of(place) == column, 1.0, 0.0).astype(jnp.bfloat16)


def take(buf, k, base):
    return jnp.concatenate([buf[k, l, pl.ds(base, 8), :] for l in range(LANES)], axis=1)


def put(buf, k, base, x):
    for l in range(LANES):
        buf[k, l, pl.ds(base, 8), :] = x[:, 128 * l : 128 * l + 128]


def put_inside(buf, k, base, x, inside):
    for l in range(LANES):
        part = slice(128 * l, 128 * l + 128)
        pltpu.store(buf.at[k, l, pl.ds(base, 8), :], x[:, part], mask=inside[:, part])


def shifted(buf, k, base, sign):
    dr, dc = sign * ROW_STEP[k], sign * COL_STEP[k]
    x = [buf[k, l, pl.ds(base + dr, 8), :] for l in range(LANES)]
    if dc == 1:
        x = x[1:] + [pltpu.roll(x[0], 127, 1)]
    if dc == -1:
        x = [pltpu.roll(x[-1], 1, 1)] + x[:-1]
    return jnp.concatenate(x, axis=1)


def mix(mat, tiles):
    x = jnp.concatenate([jnp.concatenate([p[k] for p in tiles], axis=1) for k in range(8)], axis=0)
    hi = x.astype(jnp.bfloat16)
    lo = (x - hi.astype(jnp.float32)).astype(jnp.bfloat16)
    y = jnp.dot(mat, jnp.concatenate([hi, lo], axis=0), preferred_element_type=jnp.float32)
    return [[y[8 * k : 8 * k + 8, WIDE * u : WIDE * (u + 1)] for k in range(8)] for u in range(len(tiles))]


def reach(radius):
    return (radius + 7) // 8


def span(radius):
    far = (radius + 7) // 8
    return REACH - far + 1, REACH + far + 2


def main_kernel(
    pos_ref, moves_ref, back_ref, forth_ref, hot_ref, up_ref, mid_ref, down_ref, cost_ref, values_ref, visits_ref,
    damp, start, even, odd, held, lowest, total_visits, final, stack, picked, gathered,
):
    pos = pos_ref[0]
    lane = column_of(lax.broadcasted_iota(jnp.int32, (8, WIDE), 1))
    sub = lax.broadcasted_iota(jnp.int32, (8, WIDE), 0)
    zero = jnp.zeros((8, WIDE), jnp.float32)
    one = jnp.full((8, WIDE), Z_SCALE, jnp.float32)
    for k in range(8):
        for edge in (0, TILES + 1):
            put(even, k, 8 * edge, one)
            put(odd, k, 8 * edge, one)

    def fetch(block, tile, raw):
        enter, pen = block[0:8], block[8:16]
        mass = block[16:24] if block.shape[0] == 24 else zero
        base = pl.multiple_of(8 * tile, 8)
        inside = enter > 0.0
        row = 8 * tile + sub - 8 * (REACH + 1)
        near = (row >= -20) & (row < TR + 20) & (lane >= EDGE - 20) & (lane < EDGE + TC + 20)
        start[pl.ds(base, 8), :] = jnp.where(near, mass, 0.0)
        if raw:
            damp[pl.ds(base, 8), :] = enter
            first = pen
        else:
            damp[pl.ds(base, 8), :] = jnp.where(inside, jnp.exp(-enter), 0.0)
            first = jnp.exp(pen) * Z_SCALE
        for k in range(8):
            put(even, k, base, first)
            put(odd, k, base, first)

    def load_window(raw):
        def body(tile, carry):
            at = pos + tile - 1

            below = at - REACH - GROUP

            @pl.when(at < BARE)
            def _():
                fetch(up_ref[pl.ds(pl.multiple_of(16 * at, 8), 16), :], tile, raw)

            @pl.when((at >= BARE) & (at < REACH))
            def _():
                row = pl.multiple_of(16 * BARE + 24 * (at - BARE), 8)
                fetch(up_ref[pl.ds(row, 24), :], tile, raw)

            @pl.when((at >= REACH) & (below < 0))
            def _():
                fetch(mid_ref[at - REACH], tile, raw)

            @pl.when((below >= 0) & (below < REACH - BARE))
            def _():
                fetch(down_ref[pl.ds(pl.multiple_of(24 * below, 8), 24), :], tile, raw)

            @pl.when(below >= REACH - BARE)
            def _():
                row = pl.multiple_of(24 * (REACH - BARE) + 16 * (below - REACH + BARE), 8)
                fetch(down_ref[pl.ds(row, 16), :], tile, raw)

            return carry

        lax.fori_loop(1, TILES + 1, body, 0)

    load_window(False)

    back, forth = back_ref[...], forth_ref[...]
    mine = 8 * (REACH + 1)

    center = REACH + 1

    def over_tiles(far, work):
        tiles = list(range(center - far, center + far + 1))
        for first in range(0, len(tiles), CHUNK):
            work([8 * tile for tile in tiles[first : first + CHUNK]])

    def in_pairs(first, last, sources, far, step):
        def turn(n, carry):
            step(first + 2 * n, sources[0], sources[1], far)
            step(first + 2 * n + 1, sources[1], sources[0], far)
            return carry

        lax.fori_loop(0, (last - first) // 2, turn, 0)

    def back_step(n, now, later, far):
        t = ITERS - 1 - n

        def work(bases):
            totals = mix(back, [[shifted(now, k, b, 1) for k in range(8)] for b in bases])
            for b, total in zip(bases, totals):
                e = damp[pl.ds(b, 8), :]
                inside = e > 0.0
                for k in range(8):
                    z = total[k] * e
                    put_inside(later, k, b, z, inside)
                    if b == mine:
                        held[t, k] = z

        over_tiles(far, work)

    for k in range(8):
        held[ITERS, k] = take(even, k, mine)
    in_pairs(0, 8, (even, odd), 5, back_step)
    in_pairs(8, 16, (even, odd), 4, back_step)
    in_pairs(16, 18, (even, odd), 3, back_step)
    back_step(18, even, odd, 3)
    lowest[...] = one

    def turn(bases):
        totals = mix(back, [[shifted(odd, k, b, 1) for k in range(8)] for b in bases])
        share = []
        for b, total in zip(bases, totals):
            row = b + sub - mine
            near = (row >= -20) & (row < TR + 20) & (lane >= EDGE - 20) & (lane < EDGE + TC + 20)
            live = near & (damp[pl.ds(b, 8), :] > 0.0)
            low = total[0]
            for k in range(1, 8):
                low = jnp.minimum(low, total[k])
            lowest[...] = jnp.minimum(lowest[...], jnp.where(live, low, Z_SCALE))
            mass = start[pl.ds(b, 8), :] * Y_SCALE
            live = live & (mass > 0.0)
            share.append([jnp.where(live, mass / z, 0.0) for z in total])
            if b == mine:
                for k in range(8):
                    final[8 * k : 8 * k + 8, :] = jnp.log(total[k] * (1.0 / Z_SCALE))
        flows = mix(forth, share)
        for b, flow in zip(bases, flows):
            for k in range(8):
                put(even, k, b, flow[k])

    over_tiles(3, turn)
    for k in range(8):
        for tile in (center - 4, center + 4):
            put(even, k, 8 * tile, zero)
            put(odd, k, 8 * tile, zero)
    good = jnp.min(lowest[...]) >= Z_FLOOR

    total_visits[...] = zero

    def forth_step(t, now, later, far):
        def work(bases):
            arrive = [[shifted(now, k, b, -1) for k in range(8)] for b in bases]
            if mine in bases:
                total = total_visits[...]
                for k in range(8):
                    total = total + arrive[bases.index(mine)][k] * held[t + 1, k]
                total_visits[...] = total
            damps = [damp[pl.ds(b, 8), :] for b in bases]
            flows = mix(forth, [[x * e for x in part] for e, part in zip(damps, arrive)])
            for b, flow in zip(bases, flows):
                for k in range(8):
                    put(later, k, b, flow[k])

        over_tiles(far, work)

    in_pairs(0, 4, (even, odd), 3, forth_step)
    in_pairs(4, 12, (even, odd), 2, forth_step)
    in_pairs(12, 18, (even, odd), 1, forth_step)
    forth_step(18, even, odd, 1)
    total = total_visits[...]
    for k in range(8):
        total = total + shifted(odd, k, mine, -1) * held[ITERS, k]
    final[64:72, :] = total * (1.0 / Y_SCALE)

    @pl.when(jnp.logical_not(good))
    def _():
        load_window(True)

        def log_total(h):
            most = picked[moves_ref[h, 0]]
            for a in range(1, 8):
                most = jnp.maximum(most, picked[moves_ref[h, a]])
            part = zero
            for a in range(8):
                part = part + jnp.exp(picked[moves_ref[h, a]] - most)
            return most + jnp.log(part)

        for tile in (0, TILES + 1):
            for k in range(8):
                put(even, k, 8 * tile, zero)

        def settle():
            def body(tile, carry):
                base = pl.multiple_of(8 * tile, 8)
                for k in range(8):
                    put(even, k, base, take(odd, k, base))
                return carry

            lax.fori_loop(1, TILES + 1, body, 0)

        def slow_back(n, carry):
            t = ITERS - 1 - n

            def keep(tile, carry):
                base = pl.multiple_of(8 * tile, 8)
                for k in range(8):
                    put(stack.at[n], k, pl.multiple_of(base - 16, 8), take(even, k, base))
                return carry

            lax.fori_loop(2, TILES, keep, 0)
            far = reach(t + 20)
            lo, hi = center - far, center + far + 1

            def tile_step(tile, carry):
                base = pl.multiple_of(8 * tile, 8)
                for k in range(8):
                    picked[k] = shifted(even, k, base, 1)
                enter = damp[pl.ds(base, 8), :]

                def heading(h, carry):
                    total = log_total(h)
                    put(odd, h, base, jnp.where(enter > 0.0, total - enter, 0.0))

                    @pl.when((t == 0) & (tile == REACH + 1))
                    def _():
                        final[pl.ds(pl.multiple_of(8 * h, 8), 8), :] = total

                    return carry

                return lax.fori_loop(0, 8, heading, carry)

            lax.fori_loop(lo, hi, tile_step, 0)
            settle()
            return carry

        lax.fori_loop(0, ITERS, slow_back, 0)
        for k in range(8):
            for tile in range(TILES + 2):
                put(even, k, 8 * tile, zero)
                put(odd, k, 8 * tile, zero)

        def slow_forth(t, visits):
            far = reach(ITERS - t)
            lo, hi = center - far, center + far + 1

            def tile_step(tile, carry):
                base = pl.multiple_of(8 * tile, 8)
                inside = damp[pl.ds(base, 8), :] > 0.0
                mass = start[pl.ds(base, 8), :]
                for k in range(8):
                    picked[k] = shifted(stack.at[ITERS - 1 - t], k, pl.multiple_of(base - 16, 8), 1)
                    gathered[k] = zero
                    come = jnp.where(inside, shifted(even, k, base, -1), 0.0)
                    gathered[8 + k] = jnp.where(t == 0, mass, come)

                def heading(h, carry):
                    total = log_total(h)
                    here = gathered[8 + h]
                    for a in range(8):
                        k = moves_ref[h, a]
                        gathered[k] = gathered[k] + here * jnp.exp(picked[k] - total)
                    return carry

                lax.fori_loop(0, 8, heading, 0)
                for k in range(8):
                    put(odd, k, base, gathered[k])
                return carry

            lax.fori_loop(lo, hi, tile_step, 0)
            settle()
            total = zero
            for k in range(8):
                total = total + shifted(even, k, mine, -1)
            return visits + total

        visits = lax.fori_loop(0, ITERS, slow_forth, zero)
        final[64:72, :] = visits

    out = moved(final[...], hot_ref[...])
    for k in range(8):
        values_ref[k] = (out[8 * k : 8 * k + 8] - cost_ref[...]) / ITERS
    visits_ref[...] = out[64:72]


def window_call(pos, move_table, back, forth, hot, up, mid, down, cell_cost):
    smem = pl.BlockSpec(memory_space=pltpu.SMEM)
    vmem = pl.BlockSpec(memory_space=pltpu.VMEM)
    rows = 8 * (TILES + 2)
    return pl.pallas_call(
        main_kernel,
        in_specs=[smem, smem] + [vmem] * 7,
        out_specs=[vmem, vmem],
        out_shape=[
            jax.ShapeDtypeStruct((8, TR, TC), jnp.float32),
            jax.ShapeDtypeStruct((TR, TC), jnp.float32),
        ],
        scratch_shapes=[
            pltpu.VMEM((rows, WIDE), jnp.float32),
            pltpu.VMEM((rows, WIDE), jnp.float32),
            pltpu.VMEM((8, LANES, rows, 128), jnp.float32),
            pltpu.VMEM((8, LANES, rows, 128), jnp.float32),
            pltpu.VMEM((ITERS + 1, 8, 8, WIDE), jnp.float32),
            pltpu.VMEM((8, WIDE), jnp.float32),
            pltpu.VMEM((8, WIDE), jnp.float32),
            pltpu.VMEM((72, WIDE), jnp.float32),
            pltpu.VMEM((ITERS, 8, LANES, 72, 128), jnp.float32),
            pltpu.VMEM((8, 8, WIDE), jnp.float32),
            pltpu.VMEM((16, 8, WIDE), jnp.float32),
        ],
        compiler_params=pltpu.CompilerParams(vmem_limit_bytes=50 * 2**20),
        name="raster_steps",
    )(pos, move_table, back, forth, hot, up, mid, down, cell_cost)


def prepare_call(cell_cost, blocked, cells, mass):
    edge = jax.ShapeDtypeStruct((24, WIDE), jnp.float32)
    return pl.pallas_call(
        prepare_kernel,
        out_shape=[jax.ShapeDtypeStruct((24, TC), jnp.float32), edge, edge],
        name="raster_prepare",
    )(cell_cost, blocked, cells, mass)


def aside_call(own, move_table):
    matrix = jax.ShapeDtypeStruct((64, 128), jnp.bfloat16)
    return pl.pallas_call(
        aside_kernel,
        out_shape=[
            jax.ShapeDtypeStruct((24, WIDE), jnp.float32), matrix, matrix,
            jax.ShapeDtypeStruct((WIDE, TC), jnp.bfloat16),
        ],
        cost_estimate=pl.CostEstimate(flops=2 * 72 * TC * WIDE, bytes_accessed=2**20, transcendentals=0),
        name="raster_aside",
    )(own, move_table)


def halos(mid):
    near = REACH - BARE
    above = [mid[GROUP - REACH : GROUP - near, :16].reshape(16 * BARE, WIDE), mid[GROUP - near :].reshape(24 * near, WIDE)]
    below = [mid[:near].reshape(24 * near, WIDE), mid[near:REACH, :16].reshape(16 * BARE, WIDE)]
    return jnp.concatenate(above, axis=0), jnp.concatenate(below, axis=0)


def on_device(cell_cost, blocked, move_table, anchor_cells, anchor_mass):
    n_rows, n_cols = lax.axis_size("rows"), lax.axis_size("cols")
    own, first, last = prepare_call(
        cell_cost, blocked, anchor_cells.reshape(1, 128), anchor_mass.reshape(1, 128)
    )
    left = lax.ppermute(last, "cols", [(i, i + 1) for i in range(n_cols - 1)])
    right = lax.ppermute(first, "cols", [(i + 1, i) for i in range(n_cols - 1)])
    own, back, forth, hot = aside_call(own, move_table)
    strip = own + (left + right)
    groups = [list(range(g, g + GROUP)) for g in range(0, n_rows, GROUP)]
    mid = lax.all_gather(strip, "rows", axis_index_groups=groups)
    above, below = halos(mid)
    up = lax.ppermute(above, "rows", [(i, i + GROUP) for i in range(n_rows - GROUP)])
    down = lax.ppermute(below, "rows", [(i + GROUP, i) for i in range(n_rows - GROUP)])
    pos = lax.rem(lax.axis_index("rows"), GROUP).astype(jnp.int32).reshape(1)
    values, visits = window_call(pos, move_table, back, forth, hot, up, mid, down, cell_cost)
    return values, visits


def solution(mesh):
    placed = (
        P("rows", "cols"),
        P("rows", "cols"),
        P(),
        P("rows", "cols", None),
        P("rows", "cols", None),
    )
    return jax.shard_map(
        on_device,
        mesh=mesh,
        in_specs=placed,
        out_specs=(P(None, "rows", "cols"), P("rows", "cols")),
        check_vma=False,
    )
```
